128 devices in a mesh: gx: 4 (over z), gy: 4 (over y_lo, core), gz: 8 (over y_hi, x).
Axes of the slice: x: 4, y: 4 (y_hi: 2, y_lo: 2; y = y_hi * 2 + y_lo), z: 4, core: 2. Of those that a mesh axis runs over, the one named last changes fastest.
Arguments:
- tokens: bfloat16 [2048, 18432], P(('gx', 'gy'), 'gz'), may hold values from -6 to 6
- up_weight: bfloat16 [18432, 36864], P('gz', ('gx', 'gy')), may hold values from -0.046875 to 0.046875
- down_weight: bfloat16 [36864, 18432], P(('gx', 'gy'), 'gz'), may hold values from -0.03125 to 0.03125
- readout: bfloat16 [18432], P('gz'), may hold values from -0.046875 to 0.046875
- segment_ids: int32 [2048], replicated, may hold values from 0 to 7, never falling along the last dimension, each value on 1 to 512 neighbouring positions
Outputs:
- mixed_out: bfloat16 [2048, 18432], P(('gx', 'gy'), 'gz')
- seq_scores: float32 [8], replicated
The draws below stay inside these ranges and needn't reach their ends.
Inputs may be any that keep to these rules, and one draw needn't show every extreme that they name: `segment_ids`: segment numbers never fall along the tokens; each of the 8 sequences holds 1 to 512 tokens, and one holds exactly 512.
All inputs are finite; a program needn't handle non-finite values.
Results may differ from the reference program's by a relative error of at most 0.0044.
Values may be sent and summed in bfloat16 or wider, within the bound.
A program may use at most 128 MiB of HBM per device.

```python
import math
import jax
import jax.numpy as jnp
import numpy as np
from jax import lax

D = 18432
FF = 36864
SEGS = 8
TOKENS = 2048
SEG_MOST = 512


def block_levels(key, dims, pieces, smallest, top_value):
    loudness = 1.0
    for axis_at, parts in pieces:
        draws = jax.random.uniform(jax.random.fold_in(jax.random.fold_in(key, 6), axis_at), (parts,), jnp.float32, smallest / len(pieces), top_value / len(pieces))
        loudness = loudness * jnp.repeat(jnp.exp(draws), dims[axis_at] // parts).reshape((-1,) + (1,) * (len(dims) - 1 - axis_at))
    return loudness


def profile(count, total, limit, slope):
    loads = [(1 << 20) // math.isqrt(standing ** slope) + 1 for standing in range(2, count + 1)]
    surplus, holding = total - limit - (count - 1), [1] * (count - 1)
    while surplus > 0:
        free = [i for i in range(count - 1) if holding[i] < limit]
        whole, remaining = sum([loads[i] for i in free]), surplus
        for i in free:
            addition = min(limit - holding[i], max(1, remaining * loads[i] // whole), surplus)
            holding[i] = holding[i] + addition
            surplus = surplus - addition
    return np.array([limit] + holding)


def uneven(key, amount, total, limit, skew):
    if amount == 2:
        one = jax.random.randint(key, (), max(1, total - limit), min(limit, total - 1) + 1)
        return jnp.stack([one, total - one])
    lengths = jnp.asarray(profile(amount, total, limit, skew), jnp.int32)
    twos = (amount - 1) // 2
    donor, sink = lengths[1:1 + 2 * twos:2], lengths[2:2 + 2 * twos:2]
    room = jnp.minimum(donor - 1, limit - sink)
    moved = jax.random.randint(jax.random.fold_in(key, 1), (twos,), 0, 1 << 20) % (room + 1)
    lengths = lengths.at[1:1 + 2 * twos:2].set(donor - moved).at[2:2 + 2 * twos:2].set(sink + moved)
    return lengths[jax.random.permutation(jax.random.fold_in(key, 2), amount)]


def centred(key, extent, width, reach, cuts=(), kind=jnp.bfloat16):
    gain = block_levels(key, extent, cuts, -0.22, 0.18) if cuts else 1.0
    values = jax.random.normal(key, extent, jnp.float32) * width * gain
    return jnp.minimum(jnp.maximum(values, -reach), reach).astype(kind)


def setup_inputs(seed: int = 0) -> dict:
    seeds = jax.random.split(jax.random.key(seed), 6)
    tokens = centred(seeds[0], (TOKENS, D), 1.0, 6.0, ((0, 16), (1, 8)))
    up_weight = centred(seeds[1], (D, FF), D ** -0.5, 0.046875, ((0, 8), (1, 16)))
    down_weight = centred(seeds[2], (FF, D), FF ** -0.5, 0.03125, ((0, 16), (1, 8)))
    readout = centred(seeds[3], (D,), D ** -0.5, 0.046875, ((0, 8),))
    segment_ids = jnp.searchsorted(jnp.cumsum(uneven(seeds[4], SEGS, TOKENS, SEG_MOST, 2)), jnp.arange(TOKENS), side="right").astype(jnp.int32)
    return dict(tokens=tokens, up_weight=up_weight, down_weight=down_weight, readout=readout, segment_ids=segment_ids)


def reference(tokens, up_weight, down_weight, readout, segment_ids):
    projected = jnp.dot(tokens, up_weight, preferred_element_type=jnp.float32)
    hidden = jnp.square(jnp.maximum(projected, 0.0)).astype(jnp.bfloat16)
    branch = jnp.dot(hidden, down_weight, preferred_element_type=jnp.float32)
    combined = tokens.astype(jnp.float32) + branch
    mixed_out = combined.astype(jnp.bfloat16)
    token_score = lax.optimization_barrier(jnp.sum(combined * readout.astype(jnp.float32)[None, :], axis=1))
    labels = jnp.arange(SEGS, dtype=jnp.int32)
    onehot = (segment_ids[:, None] == labels[None, :]).astype(jnp.float32)
    segment_total = lax.optimization_barrier(jnp.sum(onehot * token_score[:, None], axis=0))
    counts = lax.optimization_barrier(jnp.sum(onehot, axis=0))
    return (mixed_out, segment_total / jnp.sqrt(counts))
```

```python
import functools

import jax
import jax.numpy as jnp
from jax import lax
from jax.experimental import pallas as pl
from jax.experimental.pallas import tpu as pltpu
from jax.sharding import PartitionSpec as P

MESH = pl.DeviceIdType.MESH
SEGS = 8
PIECES = 16
CHUNK = 16
TILE = 256
PAIR_Z = (0, 1, 3, 2, 1, 3, 2, 0)
PAIR_L = (0, 0, 0, 0, 1, 1, 1, 1)
STAGES = (("own", 7), ("up", 0), ("pass", 1), ("sum", 2), ("act", 3), ("fwd", 4), ("back", 5), ("down", 6))
LAST = max(lag for _, lag in STAGES)
PART_RING = 3


def packed(table, bits):
    return sum(v << (bits * k) for k, v in enumerate(table))


def lookup(table, bits, k):
    return (packed(table, bits) >> (bits * k)) % (1 << bits)


def kernel(
    tok_hbm, up_hbm, down_hbm, read_ref, own_ids_ref, ids_ref, out_ref, score_ref,
    wu, wd, tk, pf, s1s, s2s, s1r, s2r, s3s, keep, s3r, mo, acc, xs, xr, p4s, p4r, ar1, ar2,
    w_sem, tok_sem, p1_s, p1_r, fw_s, s1_s, s1_r, s2_s, s2_r, s3_s, s3_r, s4_s, s4_r, s5_s, s5_r, s6_s, s6_r,
    x_s, x_r, p4_s, p4_r, ar1_s, ar1_r, ar2_s, ar2_r,
):
    z = lax.axis_index("gx")
    gy = lax.axis_index("gy")
    gz = lax.axis_index("gz")
    low, core = gy // 2, gy % 2
    high, x = gz // 4, gz % 4
    block = z * 4 + gy

    def in_group(gz_to):
        return (z, gy, gz_to)

    right = in_group(high * 4 + (x + 1) % 4)
    left = in_group(high * 4 + (x + 3) % 4)
    across = in_group((1 - high) * 4 + x)
    twin = (z, low * 2 + 1 - core, gz)

    def chunk(dx, j):
        at = ((x + dx) % 4) * 2 + (high + j) % 2
        return pl.ds(pl.multiple_of(at * CHUNK, CHUNK), CHUNK)

    def rcopy(src, dst, ss, rs, to):
        return pltpu.make_async_remote_copy(
            src_ref=src, dst_ref=dst, send_sem=ss, recv_sem=rs, device_id=to, device_id_type=MESH
        )

    barrier = pltpu.get_barrier_semaphore()
    for d in range(1, 8):
        pl.semaphore_signal(barrier, inc=1, device_id=in_group((gz + d) % 8), device_id_type=MESH)
    for d in range(1, 16):
        to = (block + d) % 16
        pl.semaphore_signal(barrier, inc=1, device_id=(to // 4, to % 4, gz), device_id_type=MESH)

    load_tok = pltpu.make_async_copy(tok_hbm, tk.at[0], tok_sem)
    load_up = pltpu.make_async_copy(up_hbm, wu, w_sem.at[0])
    load_down = pltpu.make_async_copy(down_hbm, wd, w_sem.at[1])
    load_tok.start()
    load_up.start()
    load_down.start()
    pl.semaphore_wait(barrier, 22)

    def gather(k):
        dz, dl = lookup(PAIR_Z, 2, k), lookup(PAIR_L, 1, k)
        to = ((z + 4 - dz) % 4, ((low + dl) % 2) * 2 + core, gz)
        return rcopy(tok_hbm, tk.at[2 * k - 1], p1_s.at[k], p1_r.at[2 * k - 1], to)

    to_twin = rcopy(tok_hbm, tk.at[15], p1_s.at[0], p1_r.at[15], twin)
    gather(1).start()
    gather(2).start()
    to_twin.start()
    load_tok.wait()
    load_up.wait()

    def forward(i):
        return rcopy(tk.at[i], tk.at[i + 1], fw_s, p1_r.at[i + 1], twin)

    def first(i, n):
        q = i % 2
        if n < 2:
            return rcopy(s1s.at[q, n], s1r.at[i, n], s1_s.at[n, q], s1_r.at[n, i], (right, left)[n])
        return rcopy(s1s.at[q, n], s2r.at[i, n - 2], s1_s.at[n, q], s2_r.at[n - 2, i], (right, left)[n - 2])

    def second(i, n):
        q = i % 2
        return rcopy(s2s.at[q, n], s2r.at[i, n + 2], s2_s.at[n, q], s2_r.at[n + 2, i], (right, left)[n])

    def third(i):
        q = i % 2
        return rcopy(s3s.at[q], s3r.at[i], s3_s.at[q], s3_r.at[i], across)

    def spread(i, dx, j, ss, rs, to):
        place = tk.at[i, chunk(dx, j)]
        return rcopy(place, place, ss, rs, to)

    def fourth(i):
        return spread(i, 0, 0, s4_s.at[i], s4_r.at[i], across)

    def fifth(i, j, n):
        return spread(i, 0, j, s5_s.at[2 * j + n, i], s5_r.at[2 * j + n, i], (right, left)[n])

    def fifth_in(i, j, n):
        return spread(i, (3, 1)[n], j, s5_s.at[2 * j + n, i], s5_r.at[2 * j + n, i], (right, left)[n])

    def sixth(i, n):
        return spread(i, (3, 1)[n], n, s6_s.at[n, i], s6_r.at[n, i], (right, left)[n])

    def sixth_in(i, n):
        return spread(i, 2, n, s6_s.at[n, i], s6_r.at[n, i], (right, left)[n])

    def exchange(k):
        return rcopy(xs, xr.at[k % 2], x_s, x_r.at[k], twin)

    def owner(k):
        dz, dl = lookup(PAIR_Z, 2, k), lookup(PAIR_L, 1, k)
        to = ((z + dz) % 4, ((low + dl) % 2) * 2 + core, gz)
        return rcopy(p4s.at[k % 2], p4r.at[k - 1], p4_s.at[k % 2], p4_r.at[k - 1], to)

    def up(i):
        @pl.when(i > 0)
        def _():
            rcopy(tk.at[i], tk.at[i], p1_s.at[0], p1_r.at[i], twin).wait_recv()

        passes = (i % 2 == 1) & (i < PIECES - 1)

        @pl.when(passes)
        def _():
            forward(i).start()

        p = i % PART_RING

        @pl.loop(0, wu.shape[1] // TILE)
        def _(n):
            cols = pl.ds(pl.multiple_of(n * TILE, TILE), TILE)
            pf[p, :, cols] = jnp.dot(tk[i], wu[:, cols], preferred_element_type=jnp.float32)

        @pl.when(i >= 2)
        def _():
            for n in range(4):
                first(i - 2, n).wait_send()

        @pl.when(passes)
        def _():
            forward(i).wait_send()

        q = i % 2
        s1s[q, 0] = pf[p, chunk(2, 0)].astype(jnp.bfloat16)
        s1s[q, 1] = pf[p, chunk(2, 1)].astype(jnp.bfloat16)
        first(i, 0).start()
        first(i, 1).start()
        s1s[q, 2] = pf[p, chunk(1, 1)].astype(jnp.bfloat16)
        s1s[q, 3] = pf[p, chunk(3, 0)].astype(jnp.bfloat16)
        first(i, 2).start()
        first(i, 3).start()

    def pass_on(i):
        p, q = i % PART_RING, i % 2

        @pl.when(i >= 2)
        def _():
            second(i - 2, 0).wait_send()
            second(i - 2, 1).wait_send()

        first(i, 0).wait_recv()
        s2s[q, 0] = (pf[p, chunk(1, 0)] + s1r[i, 0].astype(jnp.float32)).astype(jnp.bfloat16)
        second(i, 0).start()
        first(i, 1).wait_recv()
        s2s[q, 1] = (pf[p, chunk(3, 1)] + s1r[i, 1].astype(jnp.float32)).astype(jnp.bfloat16)
        second(i, 1).start()

    def sum_up(i):
        p, q = i % PART_RING, i % 2

        @pl.when(i >= 2)
        def _():
            third(i - 2).wait_send()

        first(i, 2).wait_recv()
        second(i, 1).wait_recv()
        s3s[q] = (
            pf[p, chunk(0, 1)] + s2r[i, 0].astype(jnp.float32) + s2r[i, 3].astype(jnp.float32)
        ).astype(jnp.bfloat16)
        third(i).start()
        first(i, 3).wait_recv()
        second(i, 0).wait_recv()
        keep[q] = pf[p, chunk(0, 0)] + s2r[i, 1].astype(jnp.float32) + s2r[i, 2].astype(jnp.float32)

    def act(i):
        third(i).wait_recv()
        total = keep[i % 2] + s3r[i].astype(jnp.float32)
        tk[i, chunk(0, 0)] = jnp.square(jnp.maximum(total, 0.0)).astype(jnp.bfloat16)
        fifth(i, 0, 0).start()
        fifth(i, 0, 1).start()
        fourth(i).start()

    def fwd(i):
        spread(i, 0, 1, s4_s.at[i], s4_r.at[i], across).wait_recv()
        fifth(i, 1, 0).start()
        fifth(i, 1, 1).start()
        fifth_in(i, 0, 0).wait_recv()
        sixth(i, 0).start()

    def back(i):
        fifth_in(i, 1, 1).wait_recv()
        sixth(i, 1).start()

    def down(i):
        @pl.when(i == 0)
        def _():
            load_down.wait()

        fifth_in(i, 0, 1).wait_recv()
        fifth_in(i, 1, 0).wait_recv()
        sixth_in(i, 0).wait_recv()
        sixth_in(i, 1).wait_recv()
        k = (i + 1) // 2

        def product(store):
            @pl.loop(0, wd.shape[1] // TILE)
            def _(n):
                cols = pl.ds(pl.multiple_of(n * TILE, TILE), TILE)
                store(cols, jnp.dot(tk[i], wd[:, cols], preferred_element_type=jnp.float32))

        kept = (i % 2 == 1) & (i < PIECES - 1)

        @pl.when(kept | (i == 0))
        def _():
            def store(cols, value):
                mo[k % 3, :, cols] = value

            product(store)

        @pl.when(((i % 2 == 0) & (i > 0)) | (i == PIECES - 1))
        def _():
            @pl.when(k > 1)
            def _():
                exchange(k - 1).wait_send()

            def store(cols, value):
                xs[:, cols] = value

            product(store)
            exchange(k).start()

        @pl.when(i == 0)
        def _():
            acc[...] = mo[0] + out_ref[...].astype(jnp.float32)

    def own(i):
        k = i // 2

        @pl.when((i % 2 == 0) & (i > 0))
        def _():
            exchange(k).wait_recv()

            @pl.when(k > 2)
            def _():
                owner(k - 2).wait_send()

            p4s[k % 2] = (mo[k % 3] + xr[k % 2]).astype(jnp.bfloat16)
            owner(k).start()

        fourth(i).wait_send()
        for n in range(2):
            fifth(i, 0, n).wait_send()
            fifth(i, 1, n).wait_send()
            sixth(i, n).wait_send()

    work = dict(up=up, sum=sum_up, act=act, fwd=fwd, back=back, down=down, own=own)
    work["pass"] = pass_on
    out_ref[...] = tk[0]

    @pl.loop(0, PIECES + LAST)
    def _(t):
        k = t // 2 + 2

        @pl.when((t % 2 == 0) & (t > 0) & (k < 8))
        def _():
            gather(k).start()

        for name, lag in STAGES:
            @pl.when((t >= lag) & (t < lag + PIECES))
            def _(name=name, lag=lag):
                work[name](t - lag)

    for i in (PIECES - 2, PIECES - 1):
        for n in range(4):
            first(i, n).wait_send()
        second(i, 0).wait_send()
        second(i, 1).wait_send()
        third(i).wait_send()
    to_twin.wait_send()
    for k in range(1, 8):
        gather(k).wait_send()
    owner(6).wait_send()
    owner(7).wait_send()
    exchange(8).wait_send()

    for k in range(1, 8):
        owner(k).wait_recv()
    exchange(8).wait_recv()
    lanes = lax.broadcasted_iota(jnp.int32, (CHUNK, 128), 1)
    score_ref[...] = jnp.zeros_like(score_ref)

    @pl.loop(0, PIECES // 2)
    def _(r):
        rows = pl.ds(pl.multiple_of(r * CHUNK, CHUNK), CHUNK)
        total = acc[rows] + xr[0, rows]
        for k in range(7):
            total = total + p4r[k, rows].astype(jnp.float32)
        out_ref[rows] = total.astype(jnp.bfloat16)
        score = jnp.sum(total * read_ref[...].astype(jnp.float32), axis=1, keepdims=True)
        hot = own_ids_ref[rows] == lanes
        part = jnp.sum(jnp.where(hot, score, 0.0), axis=0, keepdims=True)
        score_ref[0:1] = score_ref[0:1] + part

    ar1[gz] = score_ref[...]
    sends = []
    for d in range(1, 8):
        sends.append(rcopy(ar1.at[gz], ar1.at[gz], ar1_s.at[d], ar1_r.at[d], in_group((gz + d) % 8)))
    for s in sends:
        s.start()
    for s in sends:
        s.wait()
    part = ar1[0]
    for d in range(1, 8):
        part = part + ar1[d]
    ar2[block] = part
    sends = []
    for d in range(1, 16):
        to = (block + d) % 16
        sends.append(rcopy(ar2.at[block], ar2.at[block], ar2_s.at[d], ar2_r.at[d], (to // 4, to % 4, gz)))
    for s in sends:
        s.start()
    for s in sends:
        s.wait()
    part = ar2[0]
    for d in range(1, 16):
        part = part + ar2[d]
    ids = ids_ref[...]
    lane = lax.broadcasted_iota(jnp.int32, (8, 128), 1)
    counts = jnp.ones((8, 128), jnp.float32)
    for s in range(SEGS):
        counts = jnp.where(lane == s, jnp.sum((ids == s).astype(jnp.float32)), counts)
    score_ref[...] = part / jnp.sqrt(counts)


def per_device(tokens, up_weight, down_weight, readout, segment_ids):
    rows, width = tokens.shape
    hidden = up_weight.shape[1]
    bf16, f32 = jnp.bfloat16, jnp.float32
    offset = lax.axis_index(("gx", "gy")) * rows
    own_ids = lax.dynamic_slice_in_dim(segment_ids, offset, rows, 0)
    own_ids = jnp.broadcast_to(own_ids[:, None], (rows, 128))
    ids = segment_ids.reshape(-1, 128)
    dma = pltpu.SemaphoreType.DMA
    vmem = pl.BlockSpec(memory_space=pltpu.VMEM)
    hbm = pl.BlockSpec(memory_space=pltpu.HBM)
    mixed, scores = pl.pallas_call(
        kernel,
        out_shape=(
            jax.ShapeDtypeStruct((rows, width), bf16),
            jax.ShapeDtypeStruct((8, 128), f32),
        ),
        in_specs=[hbm, hbm, hbm, vmem, vmem, vmem],
        out_specs=(vmem, vmem),
        scratch_shapes=[
            pltpu.VMEM(up_weight.shape, bf16),
            pltpu.VMEM(down_weight.shape, bf16),
            pltpu.VMEM((PIECES, rows, width), bf16),
            pltpu.VMEM((PART_RING, rows, hidden), f32),
            pltpu.VMEM((2, 4, CHUNK, hidden), bf16),
            pltpu.VMEM((2, 2, CHUNK, hidden), bf16),
            pltpu.VMEM((PIECES, 2, CHUNK, hidden), bf16),
            pltpu.VMEM((PIECES, 4, CHUNK, hidden), bf16),
            pltpu.VMEM((2, CHUNK, hidden), bf16),
            pltpu.VMEM((2, CHUNK, hidden), f32),
            pltpu.VMEM((PIECES, CHUNK, hidden), bf16),
            pltpu.VMEM((3, rows, width), f32),
            pltpu.VMEM((rows, width), f32),
            pltpu.VMEM((rows, width), f32),
            pltpu.VMEM((2, rows, width), f32),
            pltpu.VMEM((2, rows, width), bf16),
            pltpu.VMEM((7, rows, width), bf16),
            pltpu.VMEM((8, 8, 128), f32),
            pltpu.VMEM((16, 8, 128), f32),
            dma((2,)), dma, dma((8,)), dma((PIECES,)), dma,
            dma((4, 2)), dma((2, PIECES)),
            dma((2, 2)), dma((4, PIECES)),
            dma((2,)), dma((PIECES,)),
            dma((PIECES,)), dma((PIECES,)),
            dma((4, PIECES)), dma((4, PIECES)),
            dma((2, PIECES)), dma((2, PIECES)),
            dma, dma((9,)),
            dma((2,)), dma((7,)),
            dma((8,)), dma((8,)), dma((16,)), dma((16,)),
        ],
        compiler_params=pltpu.CompilerParams(
            collective_id=0, has_side_effects=True, vmem_limit_bytes=63 * 2**20
        ),
        cost_estimate=pl.CostEstimate(
            flops=4 * PIECES * rows * width * hidden, bytes_accessed=4 * width * hidden, transcendentals=0
        ),
        name="feed_forward",
    )(tokens, up_weight, down_weight, readout.reshape(1, -1), own_ids, ids)
    return mixed, scores[0, :SEGS]


def solution(mesh):
    placed = (P(("gx", "gy"), "gz"), P("gz", ("gx", "gy")), P(("gx", "gy"), "gz"), P("gz"), P())
    return jax.shard_map(
        per_device,
        mesh=mesh,
        in_specs=placed,
        out_specs=(P(("gx", "gy"), "gz"), P()),
        check_vma=False,
    )
```

```python
import functools

import jax
import jax.numpy as jnp
from jax import lax
from jax.experimental import pallas as pl
from jax.experimental.pallas import tpu as pltpu
from jax.sharding import PartitionSpec as P

MESH = pl.DeviceIdType.MESH
SEGS = 8
PIECES = 16
CHUNK = 16
PART = 64
TILE = 768
PAIR_Z = (0, 1, 3, 2, 1, 3, 2, 0)
NEAR = 13
STAGES = (("own", 7), ("up", 0), ("pass", 1), ("sum", 2), ("act", 3), ("fwd", 4), ("back", 5), ("down", 6), ("pre", -1))
Y_FIRST = 1
LAST = max(lag for _, lag in STAGES)
PART_RING = 3


def packed(table, bits):
    return sum(v << (bits * k) for k, v in enumerate(table))


def lookup(table, bits, k):
    return (packed(table, bits) >> (bits * k)) % (1 << bits)


def kernel(
    tok_hbm, up_hbm, down_hbm, read_ref, ids_ref, out_ref, score_ref,
    wu, wd, tk, pf, s1s, s2s, s1r, s2r, s3s, y1s, keep, s3r, mo, acc, xs, xr, p4s, p4r, lane_sum, own_score, ar1, ar2,
    w_sem, tok_sem, p1_s, p1_r, fw_s, fw_r, s1_s, s1_r, s2_s, s2_r, s3_s, s3_r, s4_s, s4_r, s5_s, s5_r, s6_s, s6_r, s7_s, s7_r,
    x_s, x_r, p4_s, p4_r, ar1_s, ar1_r, ar2_s, ar2_r,
):
    z = lax.axis_index("gx")
    gy = lax.axis_index("gy")
    gz = lax.axis_index("gz")
    low, core = gy // 2, gy % 2
    high, x = gz // 4, gz % 4
    block = z * 4 + gy

    def in_group(gz_to):
        return (z, gy, gz_to)

    right = in_group(high * 4 + (x + 1) % 4)
    left = in_group(high * 4 + (x + 3) % 4)
    across = in_group((1 - high) * 4 + x)
    twin = (z, low * 2 + 1 - core, gz)

    def chunk(dx, j):
        at = ((x + dx) % 4) * 2 + (high + j) % 2
        return pl.ds(pl.multiple_of(at * CHUNK, CHUNK), CHUNK)

    def rcopy(src, dst, ss, rs, to):
        return pltpu.make_async_remote_copy(
            src_ref=src, dst_ref=dst, send_sem=ss, recv_sem=rs, device_id=to, device_id_type=MESH
        )

    barrier = pltpu.get_barrier_semaphore()
    for d in range(1, 8):
        pl.semaphore_signal(barrier, inc=1, device_id=in_group((gz + d) % 8), device_id_type=MESH)
    for d in range(1, 16):
        to = (block + d) % 16
        pl.semaphore_signal(barrier, inc=1, device_id=(to // 4, to % 4, gz), device_id_type=MESH)

    load_tok = pltpu.make_async_copy(tok_hbm, tk.at[0], tok_sem)
    load_down = pltpu.make_async_copy(down_hbm, wd, w_sem.at[0])

    def load_up(n):
        cols = pl.ds(pl.multiple_of(n * TILE, TILE), TILE)
        return pltpu.make_async_copy(up_hbm.at[:, cols], wu.at[:, cols], w_sem.at[n + 1])

    load_tok.start()
    for n in range(wu.shape[1] // TILE):
        load_up(n).start()
    pl.semaphore_wait(barrier, 22)

    def along(step):
        return ((z + step) % 4, gy, gz)

    beside = (z, (1 - low) * 2 + core, gz)

    def rows_of(part):
        return pl.ds(part * PART if isinstance(part, int) else pl.multiple_of(part * PART, PART), PART)

    mine, others = rows_of(0), rows_of(1)

    def gather(k, part):
        to, i = along(4 - lookup(PAIR_Z, 2, k)), 2 * k - 1 + part
        return rcopy(tok_hbm.at[rows_of(part)], tk.at[i, mine], p1_s.at[part, k], p1_r.at[i], to)

    def gather_near(k, part):
        to, i = along(4 - lookup(PAIR_Z, 2, k)), 2 * k - 1 + part
        return rcopy(tk.at[NEAR + part, mine], tk.at[i, mine], p1_s.at[part, k], p1_r.at[i], to)

    def to_near(part):
        i = NEAR + part
        return rcopy(tok_hbm.at[rows_of(part)], tk.at[i, mine], p1_s.at[part, 7], p1_r.at[i], beside)

    to_twin = rcopy(tok_hbm, tk.at[15], p1_s.at[0, 0], p1_r.at[15], twin)
    gather(1, 0).start()
    gather(2, 0).start()
    to_near(0).start()
    load_tok.wait()

    def forward(i):
        return rcopy(tk.at[i, mine], tk.at[i, others], fw_s, fw_r.at[i], twin)

    half = up_hbm.shape[1] // 2
    halves = (pl.ds(0, half), pl.ds(half, half))

    def first(i, n):
        q = i % 3
        if n < 2:
            return rcopy(s1s.at[q, n], s1r.at[i, n], s1_s.at[n, q], s1_r.at[n, i], (right, left)[n])
        return rcopy(s1s.at[q, n], s2r.at[i, n - 2], s1_s.at[n, q], s2_r.at[n - 2, i], (right, left)[n - 2])

    def second(i, n):
        q = i % 3
        return rcopy(s2s.at[q, n], s2r.at[i, n + 2], s2_s.at[n, q], s2_r.at[n + 2, i], (right, left)[n])

    def third(i):
        q = i % 3
        return rcopy(s3s.at[q], s3r.at[i], s3_s.at[q], s3_r.at[i], across)

    def y_first(i):
        return rcopy(y1s, s2r.at[i], s3_s.at[Y_FIRST], s3_r.at[i], across)

    def y_second(i, n):
        cols, to = halves[(0, 1, 1, 0)[n]], (right, left)[n % 2]
        dst = s3r.at[i, :, cols] if n < 2 else s1r.at[i, n - 2, :, cols]
        recv = s1_r.at[n, i] if n < 2 else s2_r.at[n - 2, i]
        return rcopy(s1s.at[Y_FIRST, (0, 0, 1, 2)[n], :, cols], dst, s1_s.at[n, Y_FIRST], recv, to)

    def y_third(i, n):
        src, dst = s1s.at[Y_FIRST, n + 1, :, halves[n]], s1r.at[i, n, :, halves[n]]
        return rcopy(src, dst, s2_s.at[n, Y_FIRST], s2_r.at[n + 2, i], (right, left)[n])

    def spread(i, dx, j, ss, rs, to):
        place = tk.at[i, chunk(dx, j)]
        return rcopy(place, place, ss, rs, to)

    def fourth(i):
        return spread(i, 0, 0, s4_s.at[i], s4_r.at[i], across)

    def fifth(i, j, n):
        return spread(i, 0, j, s5_s.at[2 * j + n, i], s5_r.at[2 * j + n, i], (right, left)[n])

    def fifth_in(i, j, n):
        return spread(i, (3, 1)[n], j, s5_s.at[2 * j + n, i], s5_r.at[2 * j + n, i], (right, left)[n])

    def sixth(i, n):
        return spread(i, (3, 1)[n], n, s6_s.at[n, i], s6_r.at[n, i], (right, left)[n])

    def sixth_in(i, n):
        return spread(i, 2, n, s6_s.at[n, i], s6_r.at[n, i], (right, left)[n])

    def y_sixth(i, n):
        place = tk.at[i, chunk((3, 1)[n], 0), halves[n]]
        return rcopy(place, place, s6_s.at[n, i], s6_r.at[n, i], (right, left)[n])

    def y_sixth_in(i, n):
        place = tk.at[i, chunk(2, 0), halves[n]]
        return rcopy(place, place, s6_s.at[n, i], s6_r.at[n, i], (right, left)[n])

    def y_last(i, n, j=0):
        if n < 2:
            return spread(i, (3, 1)[n], j, s5_s.at[2 + n, i], s5_r.at[2 + n, i], across)
        return spread(i, 2, j, s7_s.at[i], s7_r.at[i], across)

    def exchange(i):
        return rcopy(xs.at[i % 2], xr.at[i % 2], x_s.at[i % 2], x_r.at[i], twin)

    exchange_own = rcopy(xs, xr.at[pl.ds(2, 2)], x_s.at[2], x_r.at[15], twin)

    def owner(k, part):
        src, dst = p4s.at[1 - part], p4r.at[k - 1, rows_of(part)]
        return rcopy(src, dst, p4_s.at[1 - part], p4_r.at[part, k - 1], along(lookup(PAIR_Z, 2, k)))

    def owner_near(part):
        src, dst = p4s.at[1 - part], p4r.at[6, rows_of(part)]
        return rcopy(src, dst, p4_s.at[1 - part], p4_r.at[part, 6], beside)

    def pre(i):
        @pl.when((i > 0) & (i < NEAR))
        def _():
            rcopy(tk.at[i, mine], tk.at[i, mine], p1_s.at[0, 0], p1_r.at[i], twin).wait_recv()

        @pl.when((i > 0) & (i < PIECES - 1))
        def _():
            forward(i).start()

    def up(i):
        @pl.when((i > 0) & (i < PIECES - 1))
        def _():
            forward(i).wait_recv()

        @pl.when(i == PIECES - 1)
        def _():
            to_twin.wait_recv()

        p = i % PART_RING

        @pl.loop(0, wu.shape[1] // TILE)
        def _(n):
            cols = pl.ds(pl.multiple_of(n * TILE, TILE), TILE)

            @pl.when(i == 0)
            def _():
                load_up(n).wait()

            pf[p, :, cols] = jnp.dot(tk[i], wu[:, cols], preferred_element_type=jnp.float32)

        @pl.when((i > 0) & (i < PIECES - 1))
        def _():
            forward(i).wait_send()

        @pl.when((i >= NEAR) & (i < PIECES - 1))
        def _():
            for k in (4, 5, 6):
                gather_near(k, i - NEAR).wait_send()

        q = i % 3

        @pl.when(q != Y_FIRST)
        def _():
            s1s[q, 0] = pf[p, chunk(2, 0)].astype(jnp.bfloat16)
            s1s[q, 1] = pf[p, chunk(2, 1)].astype(jnp.bfloat16)
            first(i, 0).start()
            first(i, 1).start()
            s1s[q, 2] = pf[p, chunk(1, 1)].astype(jnp.bfloat16)
            s1s[q, 3] = pf[p, chunk(3, 0)].astype(jnp.bfloat16)
            first(i, 2).start()
            first(i, 3).start()

        @pl.when(q == Y_FIRST)
        def _():
            for d in range(4):
                y1s[d] = pf[p, chunk(d, 1)].astype(jnp.bfloat16)
            y_first(i).start()

    def by_kind(plain, crossed):
        def stage(i):
            pl.when(i % 3 != Y_FIRST)(lambda: plain(i))
            pl.when(i % 3 == Y_FIRST)(lambda: crossed(i))

        return stage

    def pass_on(i):
        p, q = i % PART_RING, i % 3
        first(i, 0).wait_recv()
        s2s[q, 0] = (pf[p, chunk(1, 0)] + s1r[i, 0].astype(jnp.float32)).astype(jnp.bfloat16)
        second(i, 0).start()
        first(i, 1).wait_recv()
        s2s[q, 1] = (pf[p, chunk(3, 1)] + s1r[i, 1].astype(jnp.float32)).astype(jnp.bfloat16)
        second(i, 1).start()

    def y_pass_on(i):
        p = i % PART_RING
        y_first(i).wait_recv()
        for n, d in enumerate((2, 1, 3)):
            total = pf[p, chunk(d, 0)] + s2r[i, d].astype(jnp.float32)
            s1s[Y_FIRST, n] = total.astype(jnp.bfloat16)
            if n:
                pf[p, chunk(d, 0)] = total
                y_second(i, n + 1).start()
            else:
                y_second(i, 0).start()
                y_second(i, 1).start()
        keep[Y_FIRST] = pf[p, chunk(0, 0)] + s2r[i, 0].astype(jnp.float32)
        y_first(i).wait_send()

    def sum_up(i):
        p, q = i % PART_RING, i % 3
        first(i, 2).wait_recv()
        second(i, 1).wait_recv()
        s3s[q] = (
            pf[p, chunk(0, 1)] + s2r[i, 0].astype(jnp.float32) + s2r[i, 3].astype(jnp.float32)
        ).astype(jnp.bfloat16)
        third(i).start()
        first(i, 3).wait_recv()
        second(i, 0).wait_recv()
        keep[q] = pf[p, chunk(0, 0)] + s2r[i, 1].astype(jnp.float32) + s2r[i, 2].astype(jnp.float32)
        for n in range(4):
            first(i, n).wait_send()

    def y_sum_up(i):
        p = i % PART_RING
        for n in range(2):
            cols = halves[n]
            y_second(i, n).wait_recv()
            total = pf[p, chunk((1, 3)[n], 0), cols] + s3r[i, :, cols].astype(jnp.float32)
            s1s[Y_FIRST, n + 1, :, cols] = total.astype(jnp.bfloat16)
            y_third(i, n).start()

    def act(i):
        third(i).wait_recv()
        total = keep[i % 3] + s3r[i].astype(jnp.float32)
        tk[i, chunk(0, 0)] = jnp.square(jnp.maximum(total, 0.0)).astype(jnp.bfloat16)
        fifth(i, 0, 0).start()
        fifth(i, 0, 1).start()
        fourth(i).start()
        second(i, 0).wait_send()
        second(i, 1).wait_send()

    def y_act(i):
        y_second(i, 2).wait_recv()
        y_second(i, 3).wait_recv()
        y_third(i, 0).wait_recv()
        y_third(i, 1).wait_recv()
        total = keep[Y_FIRST] + s1r[i, 0].astype(jnp.float32) + s1r[i, 1].astype(jnp.float32)
        tk[i, chunk(0, 0)] = jnp.square(jnp.maximum(total, 0.0)).astype(jnp.bfloat16)
        fifth(i, 0, 0).start()
        fifth(i, 0, 1).start()
        fourth(i).start()
        for n in range(4):
            y_second(i, n).wait_send()
        y_third(i, 0).wait_send()
        y_third(i, 1).wait_send()

    def fwd(i):
        spread(i, 0, 1, s4_s.at[i], s4_r.at[i], across).wait_recv()
        fifth(i, 1, 0).start()
        fifth(i, 1, 1).start()
        fifth_in(i, 0, 0).wait_recv()
        sixth(i, 0).start()
        third(i).wait_send()

    def y_fwd(i):
        for n in range(2):
            fifth_in(i, 0, n).wait_recv()
            y_sixth(i, n).start()
            y_last(i, n).start()

    def back(i):
        fifth_in(i, 1, 1).wait_recv()
        sixth(i, 1).start()

    def y_back(i):
        y_sixth_in(i, 0).wait_recv()
        y_sixth_in(i, 1).wait_recv()
        y_last(i, 2).start()

    def hidden_in(i):
        fifth_in(i, 0, 1).wait_recv()
        fifth_in(i, 1, 0).wait_recv()
        sixth_in(i, 0).wait_recv()
        sixth_in(i, 1).wait_recv()

    def y_hidden_in(i):
        spread(i, 0, 1, s4_s.at[i], s4_r.at[i], across).wait_recv()
        for n in range(3):
            y_last(i, n, 1).wait_recv()

    def sent(i):
        fourth(i).wait_send()
        for n in range(2):
            fifth(i, 0, n).wait_send()
            fifth(i, 1, n).wait_send()
            sixth(i, n).wait_send()

    def y_sent(i):
        fourth(i).wait_send()
        for n in range(2):
            fifth(i, 0, n).wait_send()
            y_sixth(i, n).wait_send()
        for n in range(3):
            y_last(i, n).wait_send()

    def lane_groups(value, cols):
        value = value * read_ref[:, cols].astype(jnp.float32)
        total = value[:, :128]
        for g in range(1, TILE // 128):
            total = total + value[:, g * 128 : (g + 1) * 128]
        return total

    def add_score(i, k):
        far = ((k >= 4) & (k < 8)).astype(jnp.int32)
        at = ((z + lookup(PAIR_Z, 2, k)) % 4) * 4 + ((low + far) % 2) * 2
        whole = (i == 0) | (i == PIECES - 1)
        upper = jnp.where(i == PIECES - 1, 1 - core, core)
        lower = jnp.where(i == 0, core, 1 - core)
        shape = lane_sum.shape
        row = lax.broadcasted_iota(jnp.int32, shape, 0)
        lane = lax.broadcasted_iota(jnp.int32, shape, 1)
        shift = jnp.where(whole, 0, jnp.where(row < PART, (1 - i % 2) * PART, (1 - i % 2) * PART - PART))
        names = jnp.where(
            row < PART,
            jnp.broadcast_to(ids_ref[pl.ds(at + upper, 1)], shape),
            jnp.broadcast_to(ids_ref[pl.ds(at + lower, 1)], shape),
        )
        row_ids = jnp.sum(jnp.where(lane == row + shift, names, 0), axis=1, keepdims=True)
        score = jnp.sum(lane_sum[...], axis=1, keepdims=True)
        part = jnp.sum(jnp.where(row_ids == lane, score, 0.0), axis=0, keepdims=True)
        own_score[0:1] = own_score[0:1] + part

    def down(i):
        @pl.when(i == 0)
        def _():
            load_down.wait()

        by_kind(hidden_in, y_hidden_in)(i)
        k = (i + 1) // 2
        lane_sum[...] = jnp.zeros_like(lane_sum)

        def product(store):
            @pl.loop(0, wd.shape[1] // TILE)
            def _(n):
                cols = pl.ds(pl.multiple_of(n * TILE, TILE), TILE)
                value = jnp.dot(tk[i], wd[:, cols], preferred_element_type=jnp.float32)
                store(cols, value)
                lane_sum[...] += lane_groups(value, cols)

        @pl.when(i == 0)
        def _():
            def store(cols, value):
                tokens = out_ref[:, cols].astype(jnp.float32)
                acc[:, cols] = value + tokens
                lane_sum[...] += lane_groups(tokens, cols)

            product(store)

        @pl.when((i > 0) & (i < PIECES - 1))
        def _():
            @pl.when(i > 2)
            def _():
                exchange(i - 2).wait_send()

            def store(cols, value):
                mo[i % 2, :, cols] = value[:PART]
                xs[i % 2, :, cols] = value[PART:]

            product(store)
            exchange(i).start()

        @pl.when(i == PIECES - 1)
        def _():
            exchange(i - 2).wait_send()
            exchange(i - 1).wait_send()

            def store(cols, value):
                xs[0, :, cols] = value[:PART]
                xs[1, :, cols] = value[PART:]

            product(store)
            exchange_own.start()

        add_score(i, k)

    def own(i):
        k, part = (i + 1) // 2, 1 - i % 2

        @pl.when((i > 0) & (i < NEAR))
        def _():
            exchange(i).wait_recv()

            @pl.when(i > 2)
            def _():
                owner(k - 1, part).wait_send()

            p4s[i % 2] = (mo[i % 2] + xr[i % 2]).astype(jnp.bfloat16)
            owner(k, part).start()

        @pl.when((i >= NEAR) & (i < PIECES - 1))
        def _():
            exchange(i).wait_recv()
            owner(6, part).wait_send()
            total = mo[i % 2] + xr[i % 2]
            rows = rows_of(part)
            for d in (4, 5, 6):
                owner(d, part).wait_recv()
                total = total + p4r[d - 1, rows].astype(jnp.float32)
            p4s[i % 2] = total.astype(jnp.bfloat16)
            owner_near(part).start()

        by_kind(sent, y_sent)(i)

    work = {
        "pre": pre,
        "up": up,
        "pass": by_kind(pass_on, y_pass_on),
        "sum": by_kind(sum_up, y_sum_up),
        "act": by_kind(act, y_act),
        "fwd": by_kind(fwd, y_fwd),
        "back": by_kind(back, y_back),
        "down": down,
        "own": own,
    }
    out_ref[...] = tk[0]
    own_score[...] = jnp.zeros_like(own_score)

    @pl.loop(0, PIECES + LAST)
    def _(t):
        @pl.when(t == 1)
        def _():
            to_twin.start()

        @pl.when(t == 2)
        def _():
            gather(3, 0).start()
            gather(3, 1).start()

        @pl.when(t == 4)
        def _():
            to_near(0).wait_recv()
            to_near(1).wait_recv()

        k = t // 2 + 2

        @pl.when((t % 2 == 0) & (k > 3) & (k < 7))
        def _():
            gather_near(k, 0).start()
            gather_near(k, 1).start()

        for name, lag in STAGES:
            @pl.when((t >= lag) & (t < lag + PIECES))
            def _(name=name, lag=lag):
                work[name](t - lag)

            if name == "up":

                @pl.when(t == 0)
                def _():
                    gather(1, 1).start()
                    gather(2, 1).start()
                    to_near(1).start()
                    load_down.start()


    ar1[gz] = own_score[...]
    in_sends = []
    for d in range(1, 8):
        in_sends.append(rcopy(ar1.at[gz], ar1.at[gz], ar1_s.at[d], ar1_r.at[d], in_group((gz + d) % 8)))
    for s in in_sends:
        s.start()
    to_twin.wait_send()
    for part in range(2):
        for k in (1, 2, 3):
            gather(k, part).wait_send()
        to_near(part).wait_send()
    for s in in_sends:
        s.wait()
    part = ar1[0]
    for d in range(1, 8):
        part = part + ar1[d]
    ar2[block] = part
    out_sends = []
    for d in range(1, 16):
        to = (block + d) % 16
        out_sends.append(rcopy(ar2.at[block], ar2.at[block], ar2_s.at[d], ar2_r.at[d], (to // 4, to % 4, gz)))
    for s in out_sends:
        s.start()

    for part in range(2):
        for k in (1, 2, 3):
            owner(k, part).wait_recv()
    exchange_own.wait_recv()
    owner_near(0).wait_recv()
    owner_near(1).wait_recv()

    @pl.loop(0, PIECES // 2)
    def _(r):
        rows = pl.ds(pl.multiple_of(r * CHUNK, CHUNK), CHUNK)
        at = pl.ds(pl.multiple_of(r % 4 * CHUNK, CHUNK), CHUNK)
        total = acc[rows] + xr[2 + r // 4, at]
        for k in (0, 1, 2, 6):
            total = total + p4r[k, rows].astype(jnp.float32)
        out_ref[rows] = total.astype(jnp.bfloat16)

    exchange_own.wait_send()
    owner_near(0).wait_send()
    owner_near(1).wait_send()
    for s in out_sends:
        s.wait()
    part = ar2[0]
    for d in range(1, 16):
        part = part + ar2[d]
    ids = ids_ref[...]
    lane = lax.broadcasted_iota(jnp.int32, (8, 128), 1)
    counts = jnp.ones((8, 128), jnp.float32)
    for s in range(SEGS):
        counts = jnp.where(lane == s, jnp.sum((ids == s).astype(jnp.float32)), counts)
    score_ref[...] = part / jnp.sqrt(counts)


def per_device(tokens, up_weight, down_weight, readout, segment_ids):
    rows, width = tokens.shape
    hidden = up_weight.shape[1]
    bf16, f32 = jnp.bfloat16, jnp.float32
    ids = segment_ids.reshape(-1, 128)
    dma = pltpu.SemaphoreType.DMA
    vmem = pl.BlockSpec(memory_space=pltpu.VMEM)
    hbm = pl.BlockSpec(memory_space=pltpu.HBM)
    mixed, scores = pl.pallas_call(
        kernel,
        out_shape=(
            jax.ShapeDtypeStruct((rows, width), bf16),
            jax.ShapeDtypeStruct((8, 128), f32),
        ),
        in_specs=[hbm, hbm, hbm, vmem, vmem],
        out_specs=(vmem, vmem),
        scratch_shapes=[
            pltpu.VMEM(up_weight.shape, bf16),
            pltpu.VMEM(down_weight.shape, bf16),
            pltpu.VMEM((PIECES, rows, width), bf16),
            pltpu.VMEM((PART_RING, rows, hidden), f32),
            pltpu.VMEM((3, 4, CHUNK, hidden), bf16),
            pltpu.VMEM((3, 2, CHUNK, hidden), bf16),
            pltpu.VMEM((PIECES, 2, CHUNK, hidden), bf16),
            pltpu.VMEM((PIECES, 4, CHUNK, hidden), bf16),
            pltpu.VMEM((3, CHUNK, hidden), bf16),
            pltpu.VMEM((4, CHUNK, hidden), bf16),
            pltpu.VMEM((3, CHUNK, hidden), f32),
            pltpu.VMEM((PIECES, CHUNK, hidden), bf16),
            pltpu.VMEM((2, PART, width), f32),
            pltpu.VMEM((rows, width), f32),
            pltpu.VMEM((2, PART, width), f32),
            pltpu.VMEM((4, PART, width), f32),
            pltpu.VMEM((2, PART, width), bf16),
            pltpu.VMEM((7, rows, width), bf16),
            pltpu.VMEM((rows, 128), f32),
            pltpu.VMEM((8, 128), f32),
            pltpu.VMEM((8, 8, 128), f32),
            pltpu.VMEM((16, 8, 128), f32),
            dma((1 + hidden // TILE,)), dma, dma((2, 8)), dma((PIECES,)), dma, dma((PIECES,)),
            dma((4, 3)), dma((2, PIECES)),
            dma((2, 3)), dma((4, PIECES)),
            dma((3,)), dma((PIECES,)),
            dma((PIECES,)), dma((PIECES,)),
            dma((4, PIECES)), dma((4, PIECES)),
            dma((2, PIECES)), dma((2, PIECES)),
            dma((PIECES,)), dma((PIECES,)),
            dma((3,)), dma((PIECES,)),
            dma((2,)), dma((2, 7)),
            dma((8,)), dma((8,)), dma((16,)), dma((16,)),
        ],
        compiler_params=pltpu.CompilerParams(
            collective_id=0, has_side_effects=True, vmem_limit_bytes=63 * 2**20
        ),
        cost_estimate=pl.CostEstimate(
            flops=4 * PIECES * rows * width * hidden, bytes_accessed=4 * width * hidden, transcendentals=0
        ),
        name="feed_forward",
    )(tokens, up_weight, down_weight, readout.reshape(1, -1), ids)
    return mixed, scores[0, :SEGS]


def solution(mesh):
    placed = (P(("gx", "gy"), "gz"), P("gz", ("gx", "gy")), P(("gx", "gy"), "gz"), P("gz"), P())
    return jax.shard_map(
        per_device,
        mesh=mesh,
        in_specs=placed,
        out_specs=(P(("gx", "gy"), "gz"), P()),
        check_vma=False,
    )
```

```python
import functools

import jax
import jax.numpy as jnp
from jax import lax
from jax.experimental import pallas as pl
from jax.experimental.pallas import tpu as pltpu
from jax.sharding import PartitionSpec as P

MESH = pl.DeviceIdType.MESH
SEGS = 8
PIECES = 16
CHUNK = 16
PART = 64
TILE = 768
PAIR_Z = (0, 1, 3, 2, 1, 3, 2, 0)
NEAR = 13
STAGES = (("own", 7), ("up", 0), ("pass", 1), ("sum", 2), ("act", 3), ("fwd", 4), ("back", 5), ("down", 6), ("pre", -1))
Y_FIRST = 1
LAST = max(lag for _, lag in STAGES)
PART_RING = 3


def packed(table, bits):
    return sum(v << (bits * k) for k, v in enumerate(table))


def lookup(table, bits, k):
    return (packed(table, bits) >> (bits * k)) % (1 << bits)


def kernel(
    tok_hbm, up_hbm, down_hbm, read_ref, ids_ref, out_ref, score_ref,
    wu, wd, tk, pf, s1s, s2s, s1r, s2r, s3s, y1s, keep, s3r, mo, acc, xs, xr, p4s, p4r, read_row, lane_sum, own_score, ar1, ar2,
    w_sem, tok_sem, p1_s, p1_r, fw_s, fw_r, s1_s, s1_r, s2_s, s2_r, s3_s, s3_r, s4_s, s4_r, s5_s, s5_r, s6_s, s6_r, s7_s, s7_r,
    x_s, x_r, p4_s, p4_r, ar1_s, ar1_r, ar2_s, ar2_r,
):
    z = lax.axis_index("gx")
    gy = lax.axis_index("gy")
    gz = lax.axis_index("gz")
    low, core = gy // 2, gy % 2
    high, x = gz // 4, gz % 4
    block = z * 4 + gy

    def in_group(gz_to):
        return (z, gy, gz_to)

    right = in_group(high * 4 + (x + 1) % 4)
    left = in_group(high * 4 + (x + 3) % 4)
    across = in_group((1 - high) * 4 + x)
    twin = (z, low * 2 + 1 - core, gz)

    def chunk(dx, j):
        at = ((x + dx) % 4) * 2 + (high + j) % 2
        return pl.ds(pl.multiple_of(at * CHUNK, CHUNK), CHUNK)

    def rcopy(src, dst, ss, rs, to):
        return pltpu.make_async_remote_copy(
            src_ref=src, dst_ref=dst, send_sem=ss, recv_sem=rs, device_id=to, device_id_type=MESH
        )

    barrier = pltpu.get_barrier_semaphore()
    for d in range(1, 8):
        pl.semaphore_signal(barrier, inc=1, device_id=in_group((gz + d) % 8), device_id_type=MESH)
    for d in range(1, 16):
        to = (block + d) % 16
        pl.semaphore_signal(barrier, inc=1, device_id=(to // 4, to % 4, gz), device_id_type=MESH)

    load_tok = pltpu.make_async_copy(tok_hbm, tk.at[0], tok_sem)
    load_down = pltpu.make_async_copy(down_hbm, wd, w_sem.at[0])

    def load_up(n):
        cols = pl.ds(pl.multiple_of(n * TILE, TILE), TILE)
        return pltpu.make_async_copy(up_hbm.at[:, cols], wu.at[:, cols], w_sem.at[n + 1])

    load_tok.start()
    for n in range(wu.shape[1] // TILE):
        load_up(n).start()
    pl.semaphore_wait(barrier, 22)

    def along(step):
        return ((z + step) % 4, gy, gz)

    beside = (z, (1 - low) * 2 + core, gz)

    def rows_of(part):
        return pl.ds(part * PART if isinstance(part, int) else pl.multiple_of(part * PART, PART), PART)

    mine, others = rows_of(0), rows_of(1)

    def gather(k, part):
        to, i = along(4 - lookup(PAIR_Z, 2, k)), 2 * k - 1 + part
        return rcopy(tok_hbm.at[rows_of(part)], tk.at[i, mine], p1_s.at[part, k], p1_r.at[i], to)

    def gather_near(k, part):
        to, i = along(4 - lookup(PAIR_Z, 2, k)), 2 * k - 1 + part
        return rcopy(tk.at[NEAR + part, mine], tk.at[i, mine], p1_s.at[part, k], p1_r.at[i], to)

    def to_near(part):
        i = NEAR + part
        return rcopy(tok_hbm.at[rows_of(part)], tk.at[i, mine], p1_s.at[part, 7], p1_r.at[i], beside)

    to_twin = rcopy(tok_hbm, tk.at[15], p1_s.at[0, 0], p1_r.at[15], twin)
    gather(1, 0).start()
    gather(2, 0).start()
    to_near(0).start()
    load_tok.wait()

    def forward(i):
        return rcopy(tk.at[i, mine], tk.at[i, others], fw_s, fw_r.at[i], twin)

    half = up_hbm.shape[1] // 2
    halves = (pl.ds(0, half), pl.ds(half, half))

    def first(i, n):
        q = i % 3
        if n < 2:
            return rcopy(s1s.at[q, n], s1r.at[i, n], s1_s.at[n, q], s1_r.at[n, i], (right, left)[n])
        return rcopy(s1s.at[q, n], s2r.at[i, n - 2], s1_s.at[n, q], s2_r.at[n - 2, i], (right, left)[n - 2])

    def second(i, n):
        q = i % 3
        return rcopy(s2s.at[q, n], s2r.at[i, n + 2], s2_s.at[n, q], s2_r.at[n + 2, i], (right, left)[n])

    def third(i):
        q = i % 3
        return rcopy(s3s.at[q], s3r.at[i], s3_s.at[q], s3_r.at[i], across)

    def y_first(i, n):
        if n == 0:
            return rcopy(y1s.at[0], s2r.at[i, 0], s3_s.at[Y_FIRST], s3_r.at[i], across)
        rest = pl.ds(1, 3)
        return rcopy(y1s.at[rest], s2r.at[i, rest], s1_s.at[2, Y_FIRST], s2_r.at[0, i], across)

    def y_second(i, n):
        src, dst = s1s.at[Y_FIRST, 0, :, halves[n]], s3r.at[i, :, halves[n]]
        return rcopy(src, dst, s1_s.at[n, Y_FIRST], s1_r.at[n, i], (right, left)[n])

    def y_third(i, n):
        return rcopy(s1s.at[Y_FIRST, n + 1], s1r.at[i, n], s2_s.at[n, Y_FIRST], s2_r.at[n + 2, i], (right, left)[n])

    def spread(i, dx, j, ss, rs, to):
        place = tk.at[i, chunk(dx, j)]
        return rcopy(place, place, ss, rs, to)

    def fourth(i):
        return spread(i, 0, 0, s4_s.at[i], s4_r.at[i], across)

    def fifth(i, j, n):
        return spread(i, 0, j, s5_s.at[2 * j + n, i], s5_r.at[2 * j + n, i], (right, left)[n])

    def fifth_in(i, j, n):
        return spread(i, (3, 1)[n], j, s5_s.at[2 * j + n, i], s5_r.at[2 * j + n, i], (right, left)[n])

    def sixth(i, n):
        return spread(i, (3, 1)[n], n, s6_s.at[n, i], s6_r.at[n, i], (right, left)[n])

    def sixth_in(i, n):
        return spread(i, 2, n, s6_s.at[n, i], s6_r.at[n, i], (right, left)[n])

    def y_sixth(i, n):
        place = tk.at[i, chunk((3, 1)[n], 0), halves[n]]
        return rcopy(place, place, s6_s.at[n, i], s6_r.at[n, i], (right, left)[n])

    def y_sixth_in(i, n):
        place = tk.at[i, chunk(2, 0), halves[n]]
        return rcopy(place, place, s6_s.at[n, i], s6_r.at[n, i], (right, left)[n])

    def y_last(i, n, j=0):
        if n < 2:
            return spread(i, (3, 1)[n], j, s5_s.at[2 + n, i], s5_r.at[2 + n, i], across)
        return spread(i, 2, j, s7_s.at[i], s7_r.at[i], across)

    def exchange(i):
        return rcopy(xs.at[i % 2], xr.at[i % 2], x_s.at[i % 2], x_r.at[i], twin)

    exchange_own = rcopy(xs, xr.at[pl.ds(2, 2)], x_s.at[2], x_r.at[15], twin)

    def owner(k, part):
        src, dst = p4s.at[1 - part], p4r.at[k - 1, rows_of(part)]
        return rcopy(src, dst, p4_s.at[1 - part], p4_r.at[part, k - 1], along(lookup(PAIR_Z, 2, k)))

    def owner_near(part):
        src, dst = p4s.at[1 - part], p4r.at[6, rows_of(part)]
        return rcopy(src, dst, p4_s.at[1 - part], p4_r.at[part, 6], beside)

    def pre(i):
        @pl.when((i > 0) & (i < NEAR))
        def _():
            rcopy(tk.at[i, mine], tk.at[i, mine], p1_s.at[0, 0], p1_r.at[i], twin).wait_recv()

        @pl.when((i > 0) & (i < PIECES - 1))
        def _():
            forward(i).start()

    def up(i):
        @pl.when((i > 0) & (i < PIECES - 1))
        def _():
            forward(i).wait_recv()

        @pl.when(i == PIECES - 1)
        def _():
            to_twin.wait_recv()

        p = i % PART_RING

        @pl.loop(0, wu.shape[1] // TILE)
        def _(n):
            cols = pl.ds(pl.multiple_of(n * TILE, TILE), TILE)

            @pl.when(i == 0)
            def _():
                load_up(n).wait()

            pf[p, :, cols] = jnp.dot(tk[i], wu[:, cols], preferred_element_type=jnp.float32)

        @pl.when((i > 0) & (i < PIECES - 1))
        def _():
            forward(i).wait_send()

        @pl.when((i >= NEAR) & (i < PIECES - 1))
        def _():
            for k in (4, 5, 6):
                gather_near(k, i - NEAR).wait_send()

        q = i % 3

        @pl.when(q != Y_FIRST)
        def _():
            s1s[q, 0] = pf[p, chunk(2, 0)].astype(jnp.bfloat16)
            s1s[q, 1] = pf[p, chunk(2, 1)].astype(jnp.bfloat16)
            first(i, 0).start()
            first(i, 1).start()
            s1s[q, 2] = pf[p, chunk(1, 1)].astype(jnp.bfloat16)
            s1s[q, 3] = pf[p, chunk(3, 0)].astype(jnp.bfloat16)
            first(i, 2).start()
            first(i, 3).start()

        @pl.when(q == Y_FIRST)
        def _():
            y1s[0] = pf[p, chunk(2, 1)].astype(jnp.bfloat16)
            y_first(i, 0).start()
            for n, d in enumerate((1, 3, 0)):
                y1s[n + 1] = pf[p, chunk(d, 1)].astype(jnp.bfloat16)
            y_first(i, 1).start()

    def by_kind(plain, crossed):
        def stage(i):
            pl.when(i % 3 != Y_FIRST)(lambda: plain(i))
            pl.when(i % 3 == Y_FIRST)(lambda: crossed(i))

        return stage

    def pass_on(i):
        p, q = i % PART_RING, i % 3
        first(i, 0).wait_recv()
        s2s[q, 0] = (pf[p, chunk(1, 0)] + s1r[i, 0].astype(jnp.float32)).astype(jnp.bfloat16)
        second(i, 0).start()
        first(i, 1).wait_recv()
        s2s[q, 1] = (pf[p, chunk(3, 1)] + s1r[i, 1].astype(jnp.float32)).astype(jnp.bfloat16)
        second(i, 1).start()

    def y_pass_on(i):
        y_first(i, 0).wait_recv()
        total = pf[i % PART_RING, chunk(2, 0)] + s2r[i, 0].astype(jnp.float32)
        s1s[Y_FIRST, 0] = total.astype(jnp.bfloat16)
        y_second(i, 0).start()
        y_second(i, 1).start()

    def sum_up(i):
        p, q = i % PART_RING, i % 3
        first(i, 2).wait_recv()
        second(i, 1).wait_recv()
        s3s[q] = (
            pf[p, chunk(0, 1)] + s2r[i, 0].astype(jnp.float32) + s2r[i, 3].astype(jnp.float32)
        ).astype(jnp.bfloat16)
        third(i).start()
        first(i, 3).wait_recv()
        second(i, 0).wait_recv()
        keep[q] = pf[p, chunk(0, 0)] + s2r[i, 1].astype(jnp.float32) + s2r[i, 2].astype(jnp.float32)
        for n in range(4):
            first(i, n).wait_send()

    def y_sum_up(i):
        p = i % PART_RING
        y_first(i, 1).wait_recv()
        for n in range(2):
            y_second(i, n).wait_recv()
            for h in range(2):
                cols = halves[h]
                total = pf[p, chunk((1, 3)[n], 0), cols] + s2r[i, n + 1, :, cols].astype(jnp.float32)
                if h == n:
                    total = total + s3r[i, :, cols].astype(jnp.float32)
                s1s[Y_FIRST, n + 1, :, cols] = total.astype(jnp.bfloat16)
            y_third(i, n).start()
        keep[Y_FIRST] = pf[p, chunk(0, 0)] + s2r[i, 3].astype(jnp.float32)
        y_first(i, 0).wait_send()
        y_first(i, 1).wait_send()

    def act(i):
        third(i).wait_recv()
        total = keep[i % 3] + s3r[i].astype(jnp.float32)
        tk[i, chunk(0, 0)] = jnp.square(jnp.maximum(total, 0.0)).astype(jnp.bfloat16)
        fourth(i).start()
        fifth(i, 0, 0).start()
        fifth(i, 0, 1).start()
        second(i, 0).wait_send()
        second(i, 1).wait_send()

    def y_act(i):
        y_third(i, 0).wait_recv()
        y_third(i, 1).wait_recv()
        total = keep[Y_FIRST] + s1r[i, 0].astype(jnp.float32) + s1r[i, 1].astype(jnp.float32)
        tk[i, chunk(0, 0)] = jnp.square(jnp.maximum(total, 0.0)).astype(jnp.bfloat16)
        fourth(i).start()
        fifth(i, 0, 0).start()
        fifth(i, 0, 1).start()
        for n in range(2):
            y_second(i, n).wait_send()
            y_third(i, n).wait_send()

    def fwd(i):
        spread(i, 0, 1, s4_s.at[i], s4_r.at[i], across).wait_recv()
        fifth(i, 1, 0).start()
        fifth(i, 1, 1).start()
        fifth_in(i, 0, 0).wait_recv()
        sixth(i, 0).start()
        third(i).wait_send()

    def y_fwd(i):
        for n in range(2):
            fifth_in(i, 0, n).wait_recv()
            y_sixth(i, n).start()
            y_last(i, n).start()

    def back(i):
        fifth_in(i, 1, 1).wait_recv()
        sixth(i, 1).start()

    def y_back(i):
        y_sixth_in(i, 0).wait_recv()
        y_sixth_in(i, 1).wait_recv()
        y_last(i, 2).start()

    def hidden_in(i):
        fifth_in(i, 0, 1).wait_recv()
        fifth_in(i, 1, 0).wait_recv()
        sixth_in(i, 0).wait_recv()
        sixth_in(i, 1).wait_recv()

    def y_hidden_in(i):
        spread(i, 0, 1, s4_s.at[i], s4_r.at[i], across).wait_recv()
        for n in range(3):
            y_last(i, n, 1).wait_recv()

    def sent(i):
        fourth(i).wait_send()
        for n in range(2):
            fifth(i, 0, n).wait_send()
            fifth(i, 1, n).wait_send()
            sixth(i, n).wait_send()

    def y_sent(i):
        fourth(i).wait_send()
        for n in range(2):
            fifth(i, 0, n).wait_send()
            y_sixth(i, n).wait_send()
        for n in range(3):
            y_last(i, n).wait_send()

    def lane_groups(value, cols):
        value = value * read_row[:, cols]
        total = value[:, :128]
        for g in range(1, TILE // 128):
            total = total + value[:, g * 128 : (g + 1) * 128]
        return total

    def add_score(i, k):
        far = ((k >= 4) & (k < 8)).astype(jnp.int32)
        at = ((z + lookup(PAIR_Z, 2, k)) % 4) * 4 + ((low + far) % 2) * 2
        whole = (i == 0) | (i == PIECES - 1)
        upper = jnp.where(i == PIECES - 1, 1 - core, core)
        lower = jnp.where(i == 0, core, 1 - core)
        shape = lane_sum.shape
        row = lax.broadcasted_iota(jnp.int32, shape, 0)
        lane = lax.broadcasted_iota(jnp.int32, shape, 1)
        shift = jnp.where(whole, 0, jnp.where(row < PART, (1 - i % 2) * PART, (1 - i % 2) * PART - PART))
        names = jnp.where(
            row < PART,
            jnp.broadcast_to(ids_ref[pl.ds(at + upper, 1)], shape),
            jnp.broadcast_to(ids_ref[pl.ds(at + lower, 1)], shape),
        )
        row_ids = jnp.sum(jnp.where(lane == row + shift, names, 0), axis=1, keepdims=True)
        score = jnp.sum(lane_sum[...], axis=1, keepdims=True)
        part = jnp.sum(jnp.where(row_ids == lane, score, 0.0), axis=0, keepdims=True)
        own_score[0:1] = own_score[0:1] + part

    def down(i):
        @pl.when(i == 0)
        def _():
            load_down.wait()

        by_kind(hidden_in, y_hidden_in)(i)
        k = (i + 1) // 2
        lane_sum[...] = jnp.zeros_like(lane_sum)

        def product(store):
            @pl.loop(0, wd.shape[1] // TILE)
            def _(n):
                cols = pl.ds(pl.multiple_of(n * TILE, TILE), TILE)
                value = jnp.dot(tk[i], wd[:, cols], preferred_element_type=jnp.float32)
                store(cols, value)
                lane_sum[...] += lane_groups(value, cols)

        @pl.when(i == 0)
        def _():
            def store(cols, value):
                tokens = out_ref[:, cols].astype(jnp.float32)
                acc[:, cols] = value + tokens
                lane_sum[...] += lane_groups(tokens, cols)

            product(store)

        @pl.when((i > 0) & (i < PIECES - 1))
        def _():
            @pl.when(i > 2)
            def _():
                exchange(i - 2).wait_send()

            def store(cols, value):
                mo[i % 2, :, cols] = value[:PART]
                xs[i % 2, :, cols] = value[PART:]

            product(store)
            exchange(i).start()

        @pl.when(i == PIECES - 1)
        def _():
            exchange(i - 2).wait_send()
            exchange(i - 1).wait_send()

            def store(cols, value):
                xs[0, :, cols] = value[:PART]
                xs[1, :, cols] = value[PART:]

            product(store)
            exchange_own.start()

        add_score(i, k)

    def own(i):
        k, part = (i + 1) // 2, 1 - i % 2

        @pl.when((i > 0) & (i < NEAR))
        def _():
            exchange(i).wait_recv()

            @pl.when(i > 2)
            def _():
                owner(k - 1, part).wait_send()

            p4s[i % 2] = (mo[i % 2] + xr[i % 2]).astype(jnp.bfloat16)
            owner(k, part).start()

        @pl.when((i >= NEAR) & (i < PIECES - 1))
        def _():
            exchange(i).wait_recv()
            owner(6, part).wait_send()
            total = mo[i % 2] + xr[i % 2]
            rows = rows_of(part)
            for d in (4, 5, 6):
                owner(d, part).wait_recv()
                total = total + p4r[d - 1, rows].astype(jnp.float32)
            p4s[i % 2] = total.astype(jnp.bfloat16)
            owner_near(part).start()

        by_kind(sent, y_sent)(i)

    work = {
        "pre": pre,
        "up": up,
        "pass": by_kind(pass_on, y_pass_on),
        "sum": by_kind(sum_up, y_sum_up),
        "act": by_kind(act, y_act),
        "fwd": by_kind(fwd, y_fwd),
        "back": by_kind(back, y_back),
        "down": down,
        "own": own,
    }
    out_ref[...] = tk[0]
    read_row[...] = read_ref[...].astype(jnp.float32).reshape(1, -1)
    own_score[...] = jnp.zeros_like(own_score)

    @pl.loop(0, PIECES + LAST)
    def _(t):
        @pl.when(t == 1)
        def _():
            to_twin.start()

        @pl.when(t == 2)
        def _():
            gather(3, 0).start()
            gather(3, 1).start()

        @pl.when(t == 4)
        def _():
            to_near(0).wait_recv()
            to_near(1).wait_recv()

        k = t // 2 + 2

        @pl.when((t % 2 == 0) & (k > 3) & (k < 7))
        def _():
            gather_near(k, 0).start()
            gather_near(k, 1).start()

        for name, lag in STAGES:
            @pl.when((t >= lag) & (t < lag + PIECES))
            def _(name=name, lag=lag):
                work[name](t - lag)

            if name == "up":

                @pl.when(t == 0)
                def _():
                    gather(1, 1).start()
                    gather(2, 1).start()
                    to_near(1).start()
                    load_down.start()


    ar1[gz] = own_score[...]
    in_sends = []
    for d in range(1, 8):
        in_sends.append(rcopy(ar1.at[gz], ar1.at[gz], ar1_s.at[d], ar1_r.at[d], in_group((gz + d) % 8)))
    for s in in_sends:
        s.start()
    to_twin.wait_send()
    for part in range(2):
        for k in (1, 2, 3):
            gather(k, part).wait_send()
        to_near(part).wait_send()
    for s in in_sends:
        s.wait()
    part = ar1[0]
    for d in range(1, 8):
        part = part + ar1[d]
    ar2[block] = part
    out_sends = []
    for d in range(1, 16):
        to = (block + d) % 16
        out_sends.append(rcopy(ar2.at[block], ar2.at[block], ar2_s.at[d], ar2_r.at[d], (to // 4, to % 4, gz)))
    for s in out_sends:
        s.start()

    for part in range(2):
        for k in (1, 2, 3):
            owner(k, part).wait_recv()
    exchange_own.wait_recv()
    owner_near(0).wait_recv()
    owner_near(1).wait_recv()

    @pl.loop(0, PIECES // 2)
    def _(r):
        rows = pl.ds(pl.multiple_of(r * CHUNK, CHUNK), CHUNK)
        at = pl.ds(pl.multiple_of(r % 4 * CHUNK, CHUNK), CHUNK)
        total = acc[rows] + xr[2 + r // 4, at]
        for k in (0, 1, 2, 6):
            total = total + p4r[k, rows].astype(jnp.float32)
        out_ref[rows] = total.astype(jnp.bfloat16)

    exchange_own.wait_send()
    owner_near(0).wait_send()
    owner_near(1).wait_send()
    for s in out_sends:
        s.wait()
    part = ar2[0]
    for d in range(1, 16):
        part = part + ar2[d]
    ids = ids_ref[...]
    lane = lax.broadcasted_iota(jnp.int32, (8, 128), 1)
    counts = jnp.ones((8, 128), jnp.float32)
    for s in range(SEGS):
        counts = jnp.where(lane == s, jnp.sum((ids == s).astype(jnp.float32)), counts)
    score_ref[...] = part / jnp.sqrt(counts)


def per_device(tokens, up_weight, down_weight, readout, segment_ids):
    rows, width = tokens.shape
    hidden = up_weight.shape[1]
    bf16, f32 = jnp.bfloat16, jnp.float32
    ids = segment_ids.reshape(-1, 128)
    dma = pltpu.SemaphoreType.DMA
    vmem = pl.BlockSpec(memory_space=pltpu.VMEM)
    hbm = pl.BlockSpec(memory_space=pltpu.HBM)
    mixed, scores = pl.pallas_call(
        kernel,
        out_shape=(
            jax.ShapeDtypeStruct((rows, width), bf16),
            jax.ShapeDtypeStruct((8, 128), f32),
        ),
        in_specs=[hbm, hbm, hbm, vmem, vmem],
        out_specs=(vmem, vmem),
        scratch_shapes=[
            pltpu.VMEM(up_weight.shape, bf16),
            pltpu.VMEM(down_weight.shape, bf16),
            pltpu.VMEM((PIECES, rows, width), bf16),
            pltpu.VMEM((PART_RING, rows, hidden), f32),
            pltpu.VMEM((3, 4, CHUNK, hidden), bf16),
            pltpu.VMEM((3, 2, CHUNK, hidden), bf16),
            pltpu.VMEM((PIECES, 2, CHUNK, hidden), bf16),
            pltpu.VMEM((PIECES, 4, CHUNK, hidden), bf16),
            pltpu.VMEM((3, CHUNK, hidden), bf16),
            pltpu.VMEM((4, CHUNK, hidden), bf16),
            pltpu.VMEM((3, CHUNK, hidden), f32),
            pltpu.VMEM((PIECES, CHUNK, hidden), bf16),
            pltpu.VMEM((2, PART, width), f32),
            pltpu.VMEM((rows, width), f32),
            pltpu.VMEM((2, PART, width), f32),
            pltpu.VMEM((4, PART, width), f32),
            pltpu.VMEM((2, PART, width), bf16),
            pltpu.VMEM((7, rows, width), bf16),
            pltpu.VMEM((1, width), f32),
            pltpu.VMEM((rows, 128), f32),
            pltpu.VMEM((8, 128), f32),
            pltpu.VMEM((8, 8, 128), f32),
            pltpu.VMEM((16, 8, 128), f32),
            dma((1 + hidden // TILE,)), dma, dma((2, 8)), dma((PIECES,)), dma, dma((PIECES,)),
            dma((4, 3)), dma((2, PIECES)),
            dma((2, 3)), dma((4, PIECES)),
            dma((3,)), dma((PIECES,)),
            dma((PIECES,)), dma((PIECES,)),
            dma((4, PIECES)), dma((4, PIECES)),
            dma((2, PIECES)), dma((2, PIECES)),
            dma((PIECES,)), dma((PIECES,)),
            dma((3,)), dma((PIECES,)),
            dma((2,)), dma((2, 7)),
            dma((8,)), dma((8,)), dma((16,)), dma((16,)),
        ],
        compiler_params=pltpu.CompilerParams(
            collective_id=0, has_side_effects=True, vmem_limit_bytes=63 * 2**20
        ),
        cost_estimate=pl.CostEstimate(
            flops=4 * PIECES * rows * width * hidden, bytes_accessed=4 * width * hidden, transcendentals=0
        ),
        name="feed_forward",
    )(tokens, up_weight, down_weight, readout, ids)
    return mixed, scores[0, :SEGS]


def solution(mesh):
    placed = (P(("gx", "gy"), "gz"), P("gz", ("gx", "gy")), P(("gx", "gy"), "gz"), P("gz"), P())
    return jax.shard_map(
        per_device,
        mesh=mesh,
        in_specs=placed,
        out_specs=(P(("gx", "gy"), "gz"), P()),
        check_vma=False,
    )
```

```python
import functools

import jax
import jax.numpy as jnp
from jax import lax
from jax.experimental import pallas as pl
from jax.experimental.pallas import tpu as pltpu
from jax.sharding import PartitionSpec as P

MESH = pl.DeviceIdType.MESH
SEGS = 8
PIECES = 16
CHUNK = 16
PART = 64
TILE = 768
PAIR_Z = (0, 1, 3, 2, 1, 3, 2, 0)
NEAR = 13
STAGES = (("own", 7), ("up", 0), ("pass", 1), ("sum", 2), ("act", 3), ("fwd", 4), ("back", 5), ("down", 6), ("pre", -1))
Y_FIRST = 2
LAST = max(lag for _, lag in STAGES)
PART_RING = 3


def packed(table, bits):
    return sum(v << (bits * k) for k, v in enumerate(table))


def lookup(table, bits, k):
    return (packed(table, bits) >> (bits * k)) % (1 << bits)


def kernel(
    tok_hbm, up_hbm, down_hbm, read_ref, ids_ref, out_ref, score_ref,
    wu, wd, tk, pf, s1s, s2s, s1r, s2r, s3s, y1s, keep, s3r, mo, acc, xs, xr, p4s, p4r, read_row, lane_sum, own_score, ar1, ar2,
    w_sem, tok_sem, p1_s, p1_r, fw_s, fw_r, s1_s, s1_r, s2_s, s2_r, s3_s, s3_r, s4_s, s4_r, s5_s, s5_r, s6_s, s6_r, s7_s, s7_r,
    x_s, x_r, p4_s, p4_r, ar1_s, ar1_r, ar2_s, ar2_r,
):
    z = lax.axis_index("gx")
    gy = lax.axis_index("gy")
    gz = lax.axis_index("gz")
    low, core = gy // 2, gy % 2
    high, x = gz // 4, gz % 4
    block = z * 4 + gy

    def in_group(gz_to):
        return (z, gy, gz_to)

    right = in_group(high * 4 + (x + 1) % 4)
    left = in_group(high * 4 + (x + 3) % 4)
    across = in_group((1 - high) * 4 + x)
    twin = (z, low * 2 + 1 - core, gz)

    def chunk(dx, j):
        at = ((x + dx) % 4) * 2 + (high + j) % 2
        return pl.ds(pl.multiple_of(at * CHUNK, CHUNK), CHUNK)

    def rcopy(src, dst, ss, rs, to):
        return pltpu.make_async_remote_copy(
            src_ref=src, dst_ref=dst, send_sem=ss, recv_sem=rs, device_id=to, device_id_type=MESH
        )

    barrier = pltpu.get_barrier_semaphore()
    for d in range(1, 8):
        pl.semaphore_signal(barrier, inc=1, device_id=in_group((gz + d) % 8), device_id_type=MESH)
    for d in range(1, 16):
        to = (block + d) % 16
        pl.semaphore_signal(barrier, inc=1, device_id=(to // 4, to % 4, gz), device_id_type=MESH)

    load_tok = pltpu.make_async_copy(tok_hbm, tk.at[0], tok_sem)
    load_down = pltpu.make_async_copy(down_hbm, wd, w_sem.at[0])

    def load_up(n):
        cols = pl.ds(pl.multiple_of(n * TILE, TILE), TILE)
        return pltpu.make_async_copy(up_hbm.at[:, cols], wu.at[:, cols], w_sem.at[n + 1])

    load_tok.start()
    for n in range(wu.shape[1] // TILE):
        load_up(n).start()
    pl.semaphore_wait(barrier, 22)

    def along(step):
        return ((z + step) % 4, gy, gz)

    beside = (z, (1 - low) * 2 + core, gz)

    def rows_of(part):
        return pl.ds(part * PART if isinstance(part, int) else pl.multiple_of(part * PART, PART), PART)

    mine, others = rows_of(0), rows_of(1)

    def gather(k, part):
        to, i = along(4 - lookup(PAIR_Z, 2, k)), 2 * k - 1 + part
        return rcopy(tok_hbm.at[rows_of(part)], tk.at[i, mine], p1_s.at[part, k], p1_r.at[i], to)

    def gather_near(k, part):
        to, i = along(4 - lookup(PAIR_Z, 2, k)), 2 * k - 1 + part
        return rcopy(tk.at[NEAR + part, mine], tk.at[i, mine], p1_s.at[part, k], p1_r.at[i], to)

    def to_near(part):
        i = NEAR + part
        return rcopy(tok_hbm.at[rows_of(part)], tk.at[i, mine], p1_s.at[part, 7], p1_r.at[i], beside)

    to_twin = rcopy(tok_hbm, tk.at[15], p1_s.at[0, 0], p1_r.at[15], twin)
    gather(1, 0).start()
    gather(2, 0).start()
    to_near(0).start()
    load_tok.wait()

    def forward(i):
        return rcopy(tk.at[i, mine], tk.at[i, others], fw_s, fw_r.at[i], twin)

    half = up_hbm.shape[1] // 2
    halves = (pl.ds(0, half), pl.ds(half, half))

    def first(i, n):
        q = i % 3
        if n < 2:
            return rcopy(s1s.at[q, n], s1r.at[i, n], s1_s.at[n, q], s1_r.at[n, i], (right, left)[n])
        return rcopy(s1s.at[q, n], s2r.at[i, n - 2], s1_s.at[n, q], s2_r.at[n - 2, i], (right, left)[n - 2])

    def second(i, n):
        q = i % 3
        return rcopy(s2s.at[q, n], s2r.at[i, n + 2], s2_s.at[n, q], s2_r.at[n + 2, i], (right, left)[n])

    def third(i):
        q = i % 3
        return rcopy(s3s.at[q], s3r.at[i], s3_s.at[q], s3_r.at[i], across)

    def y_first(i, n):
        if n == 0:
            return rcopy(y1s.at[0], s2r.at[i, 0], s3_s.at[Y_FIRST], s3_r.at[i], across)
        rest = pl.ds(1, 3)
        return rcopy(y1s.at[rest], s2r.at[i, rest], s1_s.at[2, Y_FIRST], s2_r.at[0, i], across)

    def y_second(i, n):
        src, dst = s1s.at[Y_FIRST, 0, :, halves[n]], s3r.at[i, :, halves[n]]
        return rcopy(src, dst, s1_s.at[n, Y_FIRST], s1_r.at[n, i], (right, left)[n])

    def y_third(i, n):
        return rcopy(s1s.at[Y_FIRST, n + 1], s1r.at[i, n], s2_s.at[n, Y_FIRST], s2_r.at[n + 2, i], (right, left)[n])

    def spread(i, dx, j, ss, rs, to):
        place = tk.at[i, chunk(dx, j)]
        return rcopy(place, place, ss, rs, to)

    def fourth(i):
        return spread(i, 0, 0, s4_s.at[i], s4_r.at[i], across)

    def fifth(i, j, n):
        return spread(i, 0, j, s5_s.at[2 * j + n, i], s5_r.at[2 * j + n, i], (right, left)[n])

    def fifth_in(i, j, n):
        return spread(i, (3, 1)[n], j, s5_s.at[2 * j + n, i], s5_r.at[2 * j + n, i], (right, left)[n])

    def sixth(i, n):
        return spread(i, (3, 1)[n], n, s6_s.at[n, i], s6_r.at[n, i], (right, left)[n])

    def sixth_in(i, n):
        return spread(i, 2, n, s6_s.at[n, i], s6_r.at[n, i], (right, left)[n])

    def y_sixth(i, n):
        place = tk.at[i, chunk((3, 1)[n], 0), halves[n]]
        return rcopy(place, place, s6_s.at[n, i], s6_r.at[n, i], (right, left)[n])

    def y_sixth_in(i, n):
        place = tk.at[i, chunk(2, 0), halves[n]]
        return rcopy(place, place, s6_s.at[n, i], s6_r.at[n, i], (right, left)[n])

    def y_last(i, n, j=0):
        if n < 2:
            return spread(i, (3, 1)[n], j, s5_s.at[2 + n, i], s5_r.at[2 + n, i], across)
        return spread(i, 2, j, s7_s.at[i], s7_r.at[i], across)

    def exchange(i):
        return rcopy(xs.at[i % 2], xr.at[i % 2], x_s.at[i % 2], x_r.at[i], twin)

    exchange_own = rcopy(xs, xr.at[pl.ds(2, 2)], x_s.at[2], x_r.at[15], twin)

    def owner(k, part):
        src, dst = p4s.at[1 - part], p4r.at[k - 1, rows_of(part)]
        return rcopy(src, dst, p4_s.at[1 - part], p4_r.at[part, k - 1], along(lookup(PAIR_Z, 2, k)))

    def owner_near(part):
        src, dst = p4s.at[1 - part], p4r.at[6, rows_of(part)]
        return rcopy(src, dst, p4_s.at[1 - part], p4_r.at[part, 6], beside)

    def pre(i):
        @pl.when((i > 0) & (i < NEAR))
        def _():
            rcopy(tk.at[i, mine], tk.at[i, mine], p1_s.at[0, 0], p1_r.at[i], twin).wait_recv()

        @pl.when((i > 0) & (i < PIECES - 1))
        def _():
            forward(i).start()

    def up(i):
        @pl.when((i > 0) & (i < PIECES - 1))
        def _():
            forward(i).wait_recv()

        @pl.when(i == PIECES - 1)
        def _():
            to_twin.wait_recv()

        p = i % PART_RING

        @pl.loop(0, wu.shape[1] // TILE)
        def _(n):
            cols = pl.ds(pl.multiple_of(n * TILE, TILE), TILE)

            @pl.when(i == 0)
            def _():
                load_up(n).wait()

            pf[p, :, cols] = jnp.dot(tk[i], wu[:, cols], preferred_element_type=jnp.float32)

        @pl.when((i > 0) & (i < PIECES - 1))
        def _():
            forward(i).wait_send()

        @pl.when((i >= NEAR) & (i < PIECES - 1))
        def _():
            for k in (4, 5, 6):
                gather_near(k, i - NEAR).wait_send()

        q = i % 3

        @pl.when(q != Y_FIRST)
        def _():
            s1s[q, 0] = pf[p, chunk(2, 0)].astype(jnp.bfloat16)
            s1s[q, 1] = pf[p, chunk(2, 1)].astype(jnp.bfloat16)
            first(i, 0).start()
            first(i, 1).start()
            s1s[q, 2] = pf[p, chunk(1, 1)].astype(jnp.bfloat16)
            s1s[q, 3] = pf[p, chunk(3, 0)].astype(jnp.bfloat16)
            first(i, 2).start()
            first(i, 3).start()

        @pl.when(q == Y_FIRST)
        def _():
            y1s[0] = pf[p, chunk(2, 1)].astype(jnp.bfloat16)
            y_first(i, 0).start()
            for n, d in enumerate((1, 3, 0)):
                y1s[n + 1] = pf[p, chunk(d, 1)].astype(jnp.bfloat16)
            y_first(i, 1).start()

    def by_kind(plain, crossed):
        def stage(i):
            pl.when(i % 3 != Y_FIRST)(lambda: plain(i))
            pl.when(i % 3 == Y_FIRST)(lambda: crossed(i))

        return stage

    def pass_on(i):
        p, q = i % PART_RING, i % 3
        first(i, 0).wait_recv()
        s2s[q, 0] = (pf[p, chunk(1, 0)] + s1r[i, 0].astype(jnp.float32)).astype(jnp.bfloat16)
        second(i, 0).start()
        first(i, 1).wait_recv()
        s2s[q, 1] = (pf[p, chunk(3, 1)] + s1r[i, 1].astype(jnp.float32)).astype(jnp.bfloat16)
        second(i, 1).start()

    def y_pass_on(i):
        y_first(i, 0).wait_recv()
        total = pf[i % PART_RING, chunk(2, 0)] + s2r[i, 0].astype(jnp.float32)
        s1s[Y_FIRST, 0] = total.astype(jnp.bfloat16)
        y_second(i, 0).start()
        y_second(i, 1).start()

    def sum_up(i):
        p, q = i % PART_RING, i % 3
        first(i, 2).wait_recv()
        second(i, 1).wait_recv()
        s3s[q] = (
            pf[p, chunk(0, 1)] + s2r[i, 0].astype(jnp.float32) + s2r[i, 3].astype(jnp.float32)
        ).astype(jnp.bfloat16)
        third(i).start()
        first(i, 3).wait_recv()
        second(i, 0).wait_recv()
        keep[q] = pf[p, chunk(0, 0)] + s2r[i, 1].astype(jnp.float32) + s2r[i, 2].astype(jnp.float32)
        for n in range(4):
            first(i, n).wait_send()

    def y_sum_up(i):
        p = i % PART_RING
        y_first(i, 1).wait_recv()
        for n in range(2):
            y_second(i, n).wait_recv()
            for h in range(2):
                cols = halves[h]
                total = pf[p, chunk((1, 3)[n], 0), cols] + s2r[i, n + 1, :, cols].astype(jnp.float32)
                if h == n:
                    total = total + s3r[i, :, cols].astype(jnp.float32)
                s1s[Y_FIRST, n + 1, :, cols] = total.astype(jnp.bfloat16)
            y_third(i, n).start()
        keep[Y_FIRST] = pf[p, chunk(0, 0)] + s2r[i, 3].astype(jnp.float32)
        y_first(i, 0).wait_send()
        y_first(i, 1).wait_send()

    def act(i):
        third(i).wait_recv()
        total = keep[i % 3] + s3r[i].astype(jnp.float32)
        tk[i, chunk(0, 0)] = jnp.square(jnp.maximum(total, 0.0)).astype(jnp.bfloat16)
        fourth(i).start()
        fifth(i, 0, 0).start()
        fifth(i, 0, 1).start()
        second(i, 0).wait_send()
        second(i, 1).wait_send()

    def y_act(i):
        y_third(i, 0).wait_recv()
        y_third(i, 1).wait_recv()
        total = keep[Y_FIRST] + s1r[i, 0].astype(jnp.float32) + s1r[i, 1].astype(jnp.float32)
        tk[i, chunk(0, 0)] = jnp.square(jnp.maximum(total, 0.0)).astype(jnp.bfloat16)
        fourth(i).start()
        fifth(i, 0, 0).start()
        fifth(i, 0, 1).start()
        for n in range(2):
            y_second(i, n).wait_send()
            y_third(i, n).wait_send()

    def fwd(i):
        spread(i, 0, 1, s4_s.at[i], s4_r.at[i], across).wait_recv()
        fifth(i, 1, 0).start()
        fifth(i, 1, 1).start()
        fifth_in(i, 0, 0).wait_recv()
        sixth(i, 0).start()
        third(i).wait_send()

    def y_fwd(i):
        for n in range(2):
            fifth_in(i, 0, n).wait_recv()
            y_sixth(i, n).start()
            y_last(i, n).start()

    def back(i):
        fifth_in(i, 1, 1).wait_recv()
        sixth(i, 1).start()

    def y_back(i):
        y_sixth_in(i, 0).wait_recv()
        y_sixth_in(i, 1).wait_recv()
        y_last(i, 2).start()

    def hidden_in(i):
        fifth_in(i, 0, 1).wait_recv()
        fifth_in(i, 1, 0).wait_recv()
        sixth_in(i, 0).wait_recv()
        sixth_in(i, 1).wait_recv()

    def y_hidden_in(i):
        spread(i, 0, 1, s4_s.at[i], s4_r.at[i], across).wait_recv()
        for n in range(3):
            y_last(i, n, 1).wait_recv()

    def sent(i):
        fourth(i).wait_send()
        for n in range(2):
            fifth(i, 0, n).wait_send()
            fifth(i, 1, n).wait_send()
            sixth(i, n).wait_send()

    def y_sent(i):
        fourth(i).wait_send()
        for n in range(2):
            fifth(i, 0, n).wait_send()
            y_sixth(i, n).wait_send()
        for n in range(3):
            y_last(i, n).wait_send()

    def lane_groups(value, cols):
        value = value * read_row[:, cols]
        total = value[:, :128]
        for g in range(1, TILE // 128):
            total = total + value[:, g * 128 : (g + 1) * 128]
        return total

    def add_score(i, k):
        far = ((k >= 4) & (k < 8)).astype(jnp.int32)
        at = ((z + lookup(PAIR_Z, 2, k)) % 4) * 4 + ((low + far) % 2) * 2
        whole = (i == 0) | (i == PIECES - 1)
        upper = jnp.where(i == PIECES - 1, 1 - core, core)
        lower = jnp.where(i == 0, core, 1 - core)
        shape = lane_sum.shape
        row = lax.broadcasted_iota(jnp.int32, shape, 0)
        lane = lax.broadcasted_iota(jnp.int32, shape, 1)
        shift = jnp.where(whole, 0, jnp.where(row < PART, (1 - i % 2) * PART, (1 - i % 2) * PART - PART))
        names = jnp.where(
            row < PART,
            jnp.broadcast_to(ids_ref[pl.ds(at + upper, 1)], shape),
            jnp.broadcast_to(ids_ref[pl.ds(at + lower, 1)], shape),
        )
        row_ids = jnp.sum(jnp.where(lane == row + shift, names, 0), axis=1, keepdims=True)
        score = jnp.sum(lane_sum[...], axis=1, keepdims=True)
        part = jnp.sum(jnp.where(row_ids == lane, score, 0.0), axis=0, keepdims=True)
        own_score[0:1] = own_score[0:1] + part

    def down(i):
        @pl.when(i == 0)
        def _():
            load_down.wait()

        by_kind(hidden_in, y_hidden_in)(i)
        k = (i + 1) // 2
        lane_sum[...] = jnp.zeros_like(lane_sum)

        def product(store):
            @pl.loop(0, wd.shape[1] // TILE)
            def _(n):
                cols = pl.ds(pl.multiple_of(n * TILE, TILE), TILE)
                value = jnp.dot(tk[i], wd[:, cols], preferred_element_type=jnp.float32)
                store(cols, value)
                lane_sum[...] += lane_groups(value, cols)

        @pl.when(i == 0)
        def _():
            def store(cols, value):
                tokens = out_ref[:, cols].astype(jnp.float32)
                acc[:, cols] = value + tokens
                lane_sum[...] += lane_groups(tokens, cols)

            product(store)

        @pl.when((i > 0) & (i < PIECES - 1))
        def _():
            @pl.when(i > 2)
            def _():
                exchange(i - 2).wait_send()

            def store(cols, value):
                mo[i % 2, :, cols] = value[:PART]
                xs[i % 2, :, cols] = value[PART:]

            product(store)
            exchange(i).start()

        @pl.when(i == PIECES - 1)
        def _():
            exchange(i - 2).wait_send()
            exchange(i - 1).wait_send()

            def store(cols, value):
                xs[0, :, cols] = value[:PART]
                xs[1, :, cols] = value[PART:]

            product(store)
            exchange_own.start()

        add_score(i, k)

    def own(i):
        k, part = (i + 1) // 2, 1 - i % 2

        @pl.when((i > 0) & (i < NEAR))
        def _():
            exchange(i).wait_recv()

            @pl.when(i > 2)
            def _():
                owner(k - 1, part).wait_send()

            p4s[i % 2] = (mo[i % 2] + xr[i % 2]).astype(jnp.bfloat16)
            owner(k, part).start()

        @pl.when((i >= NEAR) & (i < PIECES - 1))
        def _():
            exchange(i).wait_recv()
            owner(6, part).wait_send()
            total = mo[i % 2] + xr[i % 2]
            rows = rows_of(part)
            for d in (4, 5, 6):
                owner(d, part).wait_recv()
                total = total + p4r[d - 1, rows].astype(jnp.float32)
            p4s[i % 2] = total.astype(jnp.bfloat16)
            owner_near(part).start()

        by_kind(sent, y_sent)(i)

    work = {
        "pre": pre,
        "up": up,
        "pass": by_kind(pass_on, y_pass_on),
        "sum": by_kind(sum_up, y_sum_up),
        "act": by_kind(act, y_act),
        "fwd": by_kind(fwd, y_fwd),
        "back": by_kind(back, y_back),
        "down": down,
        "own": own,
    }
    out_ref[...] = tk[0]
    read_row[...] = read_ref[...].astype(jnp.float32).reshape(1, -1)
    own_score[...] = jnp.zeros_like(own_score)

    @pl.loop(0, PIECES + LAST)
    def _(t):
        @pl.when(t == 1)
        def _():
            to_twin.start()

        @pl.when(t == 2)
        def _():
            gather(3, 0).start()
            gather(3, 1).start()

        @pl.when(t == 4)
        def _():
            to_near(0).wait_recv()
            to_near(1).wait_recv()

        k = t // 2 + 2

        @pl.when((t % 2 == 0) & (k > 3) & (k < 7))
        def _():
            gather_near(k, 0).start()
            gather_near(k, 1).start()

        for name, lag in STAGES:
            @pl.when((t >= lag) & (t < lag + PIECES))
            def _(name=name, lag=lag):
                work[name](t - lag)

            if name == "up":

                @pl.when(t == 0)
                def _():
                    gather(1, 1).start()
                    gather(2, 1).start()
                    to_near(1).start()
                    load_down.start()


    ar1[gz] = own_score[...]
    in_sends = []
    for d in range(1, 8):
        in_sends.append(rcopy(ar1.at[gz], ar1.at[gz], ar1_s.at[d], ar1_r.at[d], in_group((gz + d) % 8)))
    for s in in_sends:
        s.start()
    to_twin.wait_send()
    for part in range(2):
        for k in (1, 2, 3):
            gather(k, part).wait_send()
        to_near(part).wait_send()
    for s in in_sends:
        s.wait()
    part = ar1[0]
    for d in range(1, 8):
        part = part + ar1[d]
    ar2[block] = part
    out_sends = []
    for d in range(1, 16):
        to = (block + d) % 16
        out_sends.append(rcopy(ar2.at[block], ar2.at[block], ar2_s.at[d], ar2_r.at[d], (to // 4, to % 4, gz)))
    for s in out_sends:
        s.start()

    for part in range(2):
        for k in (1, 2, 3):
            owner(k, part).wait_recv()
    exchange_own.wait_recv()
    owner_near(0).wait_recv()
    owner_near(1).wait_recv()

    @pl.loop(0, PIECES // 2)
    def _(r):
        rows = pl.ds(pl.multiple_of(r * CHUNK, CHUNK), CHUNK)
        at = pl.ds(pl.multiple_of(r % 4 * CHUNK, CHUNK), CHUNK)
        total = acc[rows] + xr[2 + r // 4, at]
        for k in (0, 1, 2, 6):
            total = total + p4r[k, rows].astype(jnp.float32)
        out_ref[rows] = total.astype(jnp.bfloat16)

    exchange_own.wait_send()
    owner_near(0).wait_send()
    owner_near(1).wait_send()
    for s in out_sends:
        s.wait()
    part = ar2[0]
    for d in range(1, 16):
        part = part + ar2[d]
    ids = ids_ref[...]
    lane = lax.broadcasted_iota(jnp.int32, (8, 128), 1)
    counts = jnp.ones((8, 128), jnp.float32)
    for s in range(SEGS):
        counts = jnp.where(lane == s, jnp.sum((ids == s).astype(jnp.float32)), counts)
    score_ref[...] = part / jnp.sqrt(counts)


def per_device(tokens, up_weight, down_weight, readout, segment_ids):
    rows, width = tokens.shape
    hidden = up_weight.shape[1]
    bf16, f32 = jnp.bfloat16, jnp.float32
    ids = segment_ids.reshape(-1, 128)
    dma = pltpu.SemaphoreType.DMA
    vmem = pl.BlockSpec(memory_space=pltpu.VMEM)
    hbm = pl.BlockSpec(memory_space=pltpu.HBM)
    mixed, scores = pl.pallas_call(
        kernel,
        out_shape=(
            jax.ShapeDtypeStruct((rows, width), bf16),
            jax.ShapeDtypeStruct((8, 128), f32),
        ),
        in_specs=[hbm, hbm, hbm, vmem, vmem],
        out_specs=(vmem, vmem),
        scratch_shapes=[
            pltpu.VMEM(up_weight.shape, bf16),
            pltpu.VMEM(down_weight.shape, bf16),
            pltpu.VMEM((PIECES, rows, width), bf16),
            pltpu.VMEM((PART_RING, rows, hidden), f32),
            pltpu.VMEM((3, 4, CHUNK, hidden), bf16),
            pltpu.VMEM((3, 2, CHUNK, hidden), bf16),
            pltpu.VMEM((PIECES, 2, CHUNK, hidden), bf16),
            pltpu.VMEM((PIECES, 4, CHUNK, hidden), bf16),
            pltpu.VMEM((3, CHUNK, hidden), bf16),
            pltpu.VMEM((4, CHUNK, hidden), bf16),
            pltpu.VMEM((3, CHUNK, hidden), f32),
            pltpu.VMEM((PIECES, CHUNK, hidden), bf16),
            pltpu.VMEM((2, PART, width), f32),
            pltpu.VMEM((rows, width), f32),
            pltpu.VMEM((2, PART, width), f32),
            pltpu.VMEM((4, PART, width), f32),
            pltpu.VMEM((2, PART, width), bf16),
            pltpu.VMEM((7, rows, width), bf16),
            pltpu.VMEM((1, width), f32),
            pltpu.VMEM((rows, 128), f32),
            pltpu.VMEM((8, 128), f32),
            pltpu.VMEM((8, 8, 128), f32),
            pltpu.VMEM((16, 8, 128), f32),
            dma((1 + hidden // TILE,)), dma, dma((2, 8)), dma((PIECES,)), dma, dma((PIECES,)),
            dma((4, 3)), dma((2, PIECES)),
            dma((2, 3)), dma((4, PIECES)),
            dma((3,)), dma((PIECES,)),
            dma((PIECES,)), dma((PIECES,)),
            dma((4, PIECES)), dma((4, PIECES)),
            dma((2, PIECES)), dma((2, PIECES)),
            dma((PIECES,)), dma((PIECES,)),
            dma((3,)), dma((PIECES,)),
            dma((2,)), dma((2, 7)),
            dma((8,)), dma((8,)), dma((16,)), dma((16,)),
        ],
        compiler_params=pltpu.CompilerParams(
            collective_id=0, has_side_effects=True, vmem_limit_bytes=63 * 2**20
        ),
        cost_estimate=pl.CostEstimate(
            flops=4 * PIECES * rows * width * hidden, bytes_accessed=4 * width * hidden, transcendentals=0
        ),
        name="feed_forward",
    )(tokens, up_weight, down_weight, readout, ids)
    return mixed, scores[0, :SEGS]


def solution(mesh):
    placed = (P(("gx", "gy"), "gz"), P("gz", ("gx", "gy")), P(("gx", "gy"), "gz"), P("gz"), P())
    return jax.shard_map(
        per_device,
        mesh=mesh,
        in_specs=placed,
        out_specs=(P(("gx", "gy"), "gz"), P()),
        check_vma=False,
    )
```
